32 devices in a mesh: grp: 4 (over y, x), seq: 8 (over z, core).
Axes of the slice: x: 2, y: 2, z: 4, core: 2. Of those that a mesh axis runs over, the one named last changes fastest.
Arguments:
- queries: bfloat16 [12288, 4096], P(('grp', 'seq')), may hold values from -6 to 6
- keys: bfloat16 [12288, 4096], P(('grp', 'seq')), may hold values from -6 to 6
- values: bfloat16 [12288, 4096], P(('grp', 'seq')), may hold values from -6 to 6
- gain: float32 [4096], replicated, may hold values from 0.5 to 1.5
Outputs:
- attended: bfloat16 [12288, 4096], P(('grp', 'seq'))
The draws below stay inside these ranges and needn't reach their ends.
All inputs are finite; a program needn't handle non-finite values.
Results may differ from the reference program's by a relative error of at most 0.0049.
Values sent between devices are 32-bit elements; how exact they have to be, the bound alone decides.
No kernel may reach another device: no remote copies, remote signals or barrier semaphores. Data moves between devices by JAX's collectives and lax.ppermute only.
A program may use at most 320 MiB of HBM per device.

```python
import jax
import jax.numpy as jnp
from jax import lax

H = 32
E = 128
TOK_DEV = 384
D = 4096
TOKENS = 12288


def levels(key, shape, split, smallest, top_value):
    def one(dim, shards_of):
        heights = jax.random.uniform(jax.random.fold_in(jax.random.fold_in(key, 6), dim), (shards_of,), jnp.float32, smallest / len(split), top_value / len(split))
        return jnp.repeat(jnp.exp(heights), shape[dim] // shards_of).reshape((-1,) + (1,) * (len(shape) - dim - 1))

    level = one(*split[0])
    for cut in split[1:]:
        level = level * one(*cut)
    return level


def normal_values(rng, shape, deviation, reach, split=(), kind=jnp.bfloat16):
    array = jax.random.normal(rng, shape, jnp.float32) * deviation
    if len(split) > 0:
        array = levels(rng, shape, split, -0.22, 0.18) * array
    return jnp.clip(array, min=-reach, max=reach).astype(kind)


def setup_inputs(seed: int = 0) -> dict:
    seeds = jax.random.split(jax.random.key(seed), 5)
    return {
        "queries": normal_values(seeds[0], (TOKENS, D), 1.0, 6.0, ((0, 32),)),
        "keys": normal_values(seeds[1], (TOKENS, D), 1.0, 6.0, ((0, 32),)),
        "values": normal_values(seeds[2], (TOKENS, D), 1.0, 6.0, ((0, 32),)),
        "gain": jnp.clip(1.0 + 0.1 * jax.random.normal(seeds[3], (D,), jnp.float32), 0.5, 1.5),
    }


def reference(queries, keys, values, gain):
    blocks = TOKENS // TOK_DEV
    qb = queries.reshape(blocks, TOK_DEV, H, E)
    kb = keys.reshape(blocks, TOK_DEV, H, E)
    vb = values.reshape(blocks, TOK_DEV, H, E)
    causal = jnp.arange(TOK_DEV)[:, None] >= jnp.arange(TOK_DEV)[None, :]
    gain_heads = gain.reshape(H, E)

    def one_block(carry, block):
        qx, kx, vx = block
        qf = qx.astype(jnp.float32)
        kf = kx.astype(jnp.float32)
        vf = vx.astype(jnp.float32)
        state = jnp.einsum('the,thf->hef', kf, vf)
        prefix_low = carry.astype(jnp.bfloat16).astype(jnp.float32)
        scores = jnp.einsum('the,she->hts', qf, kf)
        scores = jnp.where(causal[None, :, :], scores, 0.0)
        weights = scores.astype(jnp.bfloat16).astype(jnp.float32)
        mixed = jnp.einsum('hts,shf->thf', weights, vf) + jnp.einsum('the,hef->thf', qf, prefix_low)
        meansq = lax.optimization_barrier(jnp.mean(mixed * mixed, axis=-1, keepdims=True))
        normed = mixed / jnp.sqrt(meansq + 1e-06) * gain_heads[None, :, :]
        return (carry + state, normed.astype(jnp.bfloat16))
    start = jnp.zeros((H, E, E), jnp.float32)
    final, outputs = lax.scan(one_block, start, (qb, kb, vb))
    return outputs.reshape(TOKENS, D)
```

```python
import functools

import jax
import jax.numpy as jnp
from jax import lax
from jax.experimental import pallas as pl
from jax.experimental.pallas import tpu as pltpu
from jax.sharding import PartitionSpec as P

H = 32
E = 128
AXES = ("grp", "seq")
HEADS_STEP = 4
HALF = H // 2
STEPS = HALF // HEADS_STEP
WIDTH = HEADS_STEP * E


def state_kernel(half_ref, k_ref, v_ref, out_ref):
    for h in range(HEADS_STEP):
        cols = slice(h * E, (h + 1) * E)
        out_ref[cols, :] = lax.dot_general(
            k_ref[:, cols],
            v_ref[:, cols],
            (((0,), (0,)), ((), ())),
            preferred_element_type=jnp.float32,
        )


def states_of_half(half, keys, values):
    rows = keys.shape[0]
    block = pl.BlockSpec((rows, WIDTH), lambda i, half: (0, half[0] * STEPS + i))
    return pl.pallas_call(
        state_kernel,
        grid_spec=pltpu.PrefetchScalarGridSpec(
            num_scalar_prefetch=1,
            grid=(STEPS,),
            in_specs=[block, block],
            out_specs=pl.BlockSpec((WIDTH, E), lambda i, half: (i, 0)),
        ),
        out_shape=jax.ShapeDtypeStruct((HALF * E, E), jnp.float32),
        name="states",
    )(half, keys, values)


def scan_kernel(chips, x_ref, out_ref):
    rows = x_ref.shape[0] // chips
    total = jnp.zeros((rows, E), jnp.float32)
    for i in range(chips):
        part = slice(i * rows, (i + 1) * rows)
        out_ref[part, :] = total
        if i < chips - 1:
            total = total + x_ref[part, :]


def scan_chips(chips, x):
    return pl.pallas_call(
        functools.partial(scan_kernel, chips),
        in_specs=[pl.BlockSpec(memory_space=pltpu.VMEM)],
        out_specs=pl.BlockSpec(memory_space=pltpu.VMEM),
        out_shape=jax.ShapeDtypeStruct(x.shape, jnp.float32),
        name="chip_scan",
    )(x)


def mix_kernel(half_ref, q_ref, k_ref, v_ref, p_ref, gain_ref, *rest):
    out_ref = rest[-1]
    rows = q_ref.shape[0]
    tile = E
    causal = lax.broadcasted_iota(jnp.int32, (tile, tile), 0) >= lax.broadcasted_iota(
        jnp.int32, (tile, tile), 1
    )
    for h in range(HEADS_STEP):
        cols = slice(h * E, (h + 1) * E)
        low = p_ref[cols, :].astype(jnp.bfloat16)
        for r in range(rows // tile):
            here = slice(r * tile, (r + 1) * tile)
            seen = slice(0, (r + 1) * tile)
            q = q_ref[here, cols]
            scores = lax.dot_general(
                q, k_ref[seen, cols], (((1,), (1,)), ((), ())), preferred_element_type=jnp.float32
            )
            diagonal = jnp.where(causal, scores[:, r * tile :], 0.0).astype(jnp.bfloat16)
            parts = [diagonal, q]
            if r > 0:
                parts = [scores[:, : r * tile].astype(jnp.bfloat16)] + parts
            left = jnp.concatenate(parts, axis=1)
            right = jnp.concatenate([v_ref[seen, cols], low], axis=0)
            mixed = jnp.dot(left, right, preferred_element_type=jnp.float32)
            meansq = jnp.mean(mixed * mixed, axis=-1, keepdims=True)
            normed = mixed * lax.rsqrt(meansq + 1e-6) * gain_ref[:, cols]
            out_ref[here, cols] = normed.astype(jnp.bfloat16)


def mix_half(half, queries, keys, values, prefix, gain, base):
    rows = queries.shape[0]
    block = pl.BlockSpec((rows, WIDTH), lambda i, half: (0, half[0] * STEPS + i))
    in_specs = [
        block,
        block,
        block,
        pl.BlockSpec((WIDTH, E), lambda i, half: (i, 0)),
        pl.BlockSpec((1, WIDTH), lambda i, half: (0, half[0] * STEPS + i)),
    ]
    args = [half, queries, keys, values, prefix, gain]
    aliases = {}
    if base is not None:
        in_specs.append(pl.BlockSpec(memory_space=pl.ANY))
        args.append(base)
        aliases = {len(args) - 1: 0}
    return pl.pallas_call(
        mix_kernel,
        grid_spec=pltpu.PrefetchScalarGridSpec(
            num_scalar_prefetch=1, grid=(STEPS,), in_specs=in_specs, out_specs=block
        ),
        out_shape=jax.ShapeDtypeStruct(queries.shape, jnp.bfloat16),
        input_output_aliases=aliases,
        name="mix",
    )(*args)


def shards(queries, keys, values, gain):
    devices = lax.axis_size("grp") * lax.axis_size("seq")
    chips = devices // 2
    core = lax.rem(lax.axis_index("seq"), 2).astype(jnp.int32)
    mine, other = core.reshape(1), (1 - core).reshape(1)
    sibling = [(i, i ^ 1) for i in range(devices)]
    groups = [[2 * i + c for i in range(chips)] for c in (0, 1)]
    gain = gain.reshape(1, H * E)

    send = states_of_half(other, keys, values)
    got = lax.ppermute(send, AXES, sibling)
    keep = states_of_half(mine, keys, values)
    chip = keep + got
    everyone = lax.all_to_all(chip, AXES, 0, 0, axis_index_groups=groups, tiled=True)
    before = scan_chips(chips, everyone)
    before = lax.all_to_all(before, AXES, 0, 0, axis_index_groups=groups, tiled=True)
    second = core == 1
    to_sibling = before + jnp.where(second, 0.0, keep)
    prefix_mine = before + jnp.where(second, got, 0.0)
    prefix_other = lax.ppermute(to_sibling, AXES, sibling)
    out = mix_half(mine, queries, keys, values, prefix_mine, gain, None)
    return mix_half(other, queries, keys, values, prefix_other, gain, out)


def solution(mesh):
    rows = P(("grp", "seq"), None)
    return jax.shard_map(
        shards, mesh=mesh, in_specs=(rows, rows, rows, P()), out_specs=rows, check_vma=False
    )
```

```python
import functools

import jax
import jax.numpy as jnp
from jax import lax
from jax.experimental import pallas as pl
from jax.experimental.pallas import tpu as pltpu
from jax.sharding import PartitionSpec as P

H = 32
E = 128
AXES = ("grp", "seq")
HALF = H // 2
PIECE = 4
WIDTH = PIECE * E
VMEM = pl.BlockSpec(memory_space=pltpu.VMEM)
SMEM = pl.BlockSpec(memory_space=pltpu.SMEM)
HBM = pl.BlockSpec(memory_space=pltpu.HBM)


def limit(mebibytes):
    return pltpu.CompilerParams(vmem_limit_bytes=mebibytes * 1024 * 1024)


def in_vmem(x):
    return pltpu.with_memory_space_constraint(x, pltpu.VMEM)


def in_hbm(x):
    return pltpu.with_memory_space_constraint(x, pltpu.HBM)


def lane_tile(start, size):
    return pl.ds(pl.multiple_of(start, E), size)


def state_kernel(first_ref, k_ref, v_ref, out_ref, k_buf, v_buf, sems):
    heads = out_ref.shape[0] // E
    base = first_ref[0] * E
    copies = []
    for piece in range(heads // PIECE):
        for n, (ref, buf) in enumerate(((k_ref, k_buf), (v_ref, v_buf))):
            copy = pltpu.make_async_copy(
                ref.at[:, lane_tile(base + piece * WIDTH, WIDTH)],
                buf.at[piece],
                sems.at[n, piece],
            )
            copy.start()
            copies.append(copy)
    for piece in range(heads // PIECE):
        copies[2 * piece].wait()
        copies[2 * piece + 1].wait()
        for h in range(PIECE):
            cols = slice(h * E, (h + 1) * E)
            here = (piece * PIECE + h) * E
            out_ref[here : here + E, :] = lax.dot_general(
                k_buf[piece, :, cols],
                v_buf[piece, :, cols],
                (((0,), (0,)), ((), ())),
                preferred_element_type=jnp.float32,
            )


def states_of(first, heads, keys, values):
    rows = keys.shape[0]
    pieces = heads // PIECE
    return pl.pallas_call(
        state_kernel,
        in_specs=[SMEM, HBM, HBM],
        out_specs=VMEM,
        out_shape=pltpu.VMEM((heads * E, E), jnp.float32),
        scratch_shapes=[
            pltpu.VMEM((pieces, rows, WIDTH), jnp.bfloat16),
            pltpu.VMEM((pieces, rows, WIDTH), jnp.bfloat16),
            pltpu.SemaphoreType.DMA((2, pieces)),
        ],
        compiler_params=limit(6),
        name="states",
    )(first, in_hbm(keys), in_hbm(values))


def pair_kernel(core_ref, keep_ref, got_ref, chip_ref, first_ref, chip_buf, first_buf, sems):
    rows = chip_buf.shape[1]
    copies = []
    for piece in range(chip_buf.shape[0]):
        part = slice(piece * rows, (piece + 1) * rows)
        keep, got = keep_ref[part, :], got_ref[part, :]
        chip_buf[piece] = keep + got
        first_buf[piece] = jnp.where(core_ref[0] == 0, keep, got)
        for n, (buf, ref) in enumerate(((chip_buf, chip_ref), (first_buf, first_ref))):
            copy = pltpu.make_async_copy(buf.at[piece], ref.at[part, :], sems.at[n, piece])
            copy.start()
            copies.append(copy)
    for copy in copies:
        copy.wait()


def pair_states(core, keep, got):
    shape = pltpu.HBM(keep.shape, jnp.float32)
    buf = pltpu.VMEM((PIECE, keep.shape[0] // PIECE, E), jnp.float32)
    return pl.pallas_call(
        pair_kernel,
        in_specs=[SMEM, VMEM, VMEM],
        out_specs=(HBM, HBM),
        out_shape=(shape, shape),
        scratch_shapes=[buf, buf, pltpu.SemaphoreType.DMA((2, PIECE))],
        compiler_params=limit(6),
        name="pair",
    )(core, in_vmem(keep), in_vmem(got))


def shift_kernel(core_ref, before_ref, first_ref, out_ref):
    add = (core_ref[0] == 0).astype(jnp.float32)
    out_ref[...] = before_ref[...] + add * first_ref[...]


def for_sibling(core, before, first):
    return pl.pallas_call(
        shift_kernel,
        in_specs=[SMEM, VMEM, VMEM],
        out_specs=VMEM,
        out_shape=pltpu.VMEM(before.shape, jnp.float32),
        compiler_params=limit(6),
        name="for_sibling",
    )(core, in_vmem(before), in_vmem(first))


def scan_kernel(chips, x_ref, out_ref):
    rows = x_ref.shape[0] // chips
    total = jnp.zeros((rows, E), jnp.float32)
    for i in range(chips):
        part = slice(i * rows, (i + 1) * rows)
        out_ref[part, :] = total
        if i < chips - 1:
            total = total + x_ref[part, :]


def scan_chips(chips, x):
    return pl.pallas_call(
        functools.partial(scan_kernel, chips),
        in_specs=[VMEM],
        out_specs=VMEM,
        out_shape=pltpu.VMEM(x.shape, jnp.float32),
        compiler_params=limit(4),
        name="chip_scan",
    )(in_vmem(x))


def local_kernel(q_ref, k_ref, v_ref, out_ref):
    rows, width = q_ref.shape
    causal = lax.broadcasted_iota(jnp.int32, (rows, rows), 0) >= lax.broadcasted_iota(
        jnp.int32, (rows, rows), 1
    )
    for h in range(width // E):
        cols = slice(h * E, (h + 1) * E)
        scores = lax.dot_general(
            q_ref[:, cols],
            k_ref[:, cols],
            (((1,), (1,)), ((), ())),
            preferred_element_type=jnp.float32,
        )
        weights = jnp.where(causal, scores, 0.0).astype(jnp.bfloat16)
        out_ref[:, cols] = jnp.dot(weights, v_ref[:, cols], preferred_element_type=jnp.float32)


def local_mix(queries, keys, values):
    rows, width = queries.shape
    block = pl.BlockSpec((rows, 8 * E), lambda i: (0, i))
    return pl.pallas_call(
        local_kernel,
        grid=(width // (8 * E),),
        in_specs=[block, block, block],
        out_specs=block,
        out_shape=pltpu.HBM(queries.shape, jnp.float32),
        compiler_params=limit(24),
        name="local",
    )(queries, keys, values)


def finish_kernel(core_ref, q_ref, m_ref, p_ref, first_ref, gain_ref, *rest):
    out_ref, buf, sems = rest[-3:]
    heads = p_ref.shape[0] // E
    base = core_ref[0] * E
    stores = []
    for piece in range(heads // PIECE):
        for h in range(PIECE):
            here = (piece * PIECE + h) * E
            cols = lane_tile(base + here, E)
            low = p_ref[here : here + E, :]
            if first_ref is not None:
                low = low + core_ref[1].astype(jnp.float32) * first_ref[here : here + E, :]
            mixed = m_ref[:, cols] + jnp.dot(
                q_ref[:, cols], low.astype(jnp.bfloat16), preferred_element_type=jnp.float32
            )
            meansq = jnp.mean(mixed * mixed, axis=-1, keepdims=True)
            normed = mixed * lax.rsqrt(meansq + 1e-6) * gain_ref[:, cols]
            buf[piece, :, h * E : (h + 1) * E] = normed.astype(jnp.bfloat16)
        copy = pltpu.make_async_copy(
            buf.at[piece], out_ref.at[:, lane_tile(base + piece * WIDTH, WIDTH)], sems.at[piece]
        )
        copy.start()
        stores.append(copy)
    for copy in stores:
        copy.wait()


def finish_mine_kernel(core_ref, q_ref, m_ref, p_ref, first_ref, gain_ref, *rest):
    finish_kernel(core_ref, q_ref, m_ref, p_ref, first_ref, gain_ref, *rest)


def finish_other_kernel(core_ref, q_ref, m_ref, p_ref, gain_ref, *rest):
    finish_kernel(core_ref, q_ref, m_ref, p_ref, None, gain_ref, *rest)


def finish(core, queries, mixed, prefix, first, gain, base):
    rows = queries.shape[0]
    pieces = prefix.shape[0] // E // PIECE
    args = [core, in_vmem(queries), in_vmem(mixed), in_vmem(prefix)]
    in_specs = [SMEM, VMEM, VMEM, VMEM]
    if first is not None:
        args.append(in_vmem(first))
        in_specs.append(VMEM)
    args.append(gain)
    in_specs.append(VMEM)
    aliases = {}
    if base is not None:
        in_specs.append(HBM)
        args.append(in_hbm(base))
        aliases = {len(args) - 1: 0}
    return pl.pallas_call(
        finish_other_kernel if first is None else finish_mine_kernel,
        in_specs=in_specs,
        out_specs=HBM,
        out_shape=pltpu.HBM(queries.shape, jnp.bfloat16),
        scratch_shapes=[
            pltpu.VMEM((pieces, rows, WIDTH), jnp.bfloat16),
            pltpu.SemaphoreType.DMA((pieces,)),
        ],
        input_output_aliases=aliases,
        compiler_params=limit(6),
        name="finish",
    )(*args)


def shards(queries, keys, values, gain):
    devices = lax.axis_size("grp") * lax.axis_size("seq")
    chips = devices // 2
    core = lax.rem(lax.axis_index("seq"), 2).astype(jnp.int32)
    sibling = [(i, i ^ 1) for i in range(devices)]
    groups = [[2 * i + c for i in range(chips)] for c in (0, 1)]
    gain = gain.reshape(1, H * E)
    which = core.reshape(1)
    mine = jnp.stack([core * HALF, core])
    other = jnp.stack([(1 - core) * HALF, core])

    def exchange(x):
        return lax.all_to_all(x, AXES, 0, 0, axis_index_groups=groups, tiled=True)

    send = states_of(other, HALF, keys, values)
    got = lax.ppermute(send, AXES, sibling)
    keep = states_of(mine, HALF, keys, values)
    chip, first = pair_states(which, keep, got)
    chip, queries = lax.optimization_barrier((chip, queries))
    everyone = exchange(chip)
    mixed = local_mix(in_hbm(queries), in_hbm(keys), in_hbm(values))
    everyone, mixed = lax.optimization_barrier((everyone, mixed))
    before = exchange(scan_chips(chips, everyone))
    prefix_other = lax.ppermute(for_sibling(which, before, first), AXES, sibling)
    out = finish(mine, queries, mixed, before, first, gain, None)
    return finish(other, queries, mixed, prefix_other, None, gain, out)


def solution(mesh):
    rows = P(("grp", "seq"), None)
    return jax.shard_map(
        shards, mesh=mesh, in_specs=(rows, rows, rows, P()), out_specs=rows, check_vma=False
    )
```

```python
import functools

import jax
import jax.numpy as jnp
from jax import lax
from jax.experimental import pallas as pl
from jax.experimental.pallas import tpu as pltpu
from jax.sharding import PartitionSpec as P

H = 32
E = 128
AXES = ("grp", "seq")
HALF = H // 2
CHUNKS = 2
HEADS = HALF // CHUNKS
PIECE = 4
WIDTH = PIECE * E


def limit(mebibytes):
    return pltpu.CompilerParams(vmem_limit_bytes=mebibytes * 1024 * 1024)


def lane_tile(start, size):
    return pl.ds(pl.multiple_of(start, E), size)


def bit_of(level):
    index, length = lax.axis_index("seq"), lax.axis_size("seq")
    levels = length.bit_length() - 1
    if level < levels:
        return (index >> level) & 1
    return (lax.axis_index("grp") >> (level - levels)) & 1


def first_column(chunk, mine):
    core = bit_of(0)
    half = core if mine else 1 - core
    return (half * HALF + chunk * HEADS) * E


def state_kernel(chunk, mine, k_ref, v_ref, out_ref, k_buf, v_buf, sems):
    base = first_column(chunk, mine)
    copies = []
    for piece in range(HEADS // PIECE):
        for n, (ref, buf) in enumerate(((k_ref, k_buf), (v_ref, v_buf))):
            copy = pltpu.make_async_copy(
                ref.at[:, lane_tile(base + piece * WIDTH, WIDTH)],
                buf.at[piece],
                sems.at[n, piece],
            )
            copy.start()
            copies.append(copy)
    for piece in range(HEADS // PIECE):
        copies[2 * piece].wait()
        copies[2 * piece + 1].wait()
        for h in range(PIECE):
            cols = slice(h * E, (h + 1) * E)
            here = (piece * PIECE + h) * E
            out_ref[here : here + E, :] = lax.dot_general(
                k_buf[piece, :, cols],
                v_buf[piece, :, cols],
                (((0,), (0,)), ((), ())),
                preferred_element_type=jnp.float32,
            )


def call(kernel, name, arrays, shapes, scratch=(), tie=(), alias=None, mebibytes=4):
    count, operands = len(arrays), list(arrays) + list(tie)

    def body(*refs):
        kernel(*refs[:count], *refs[len(operands) :])

    return pl.pallas_call(
        body,
        in_specs=[pl.BlockSpec(memory_space=space) for _, space in operands],
        out_specs=tuple(pl.BlockSpec(memory_space=space) for space, _, _ in shapes),
        out_shape=tuple(space(shape, kind) for space, shape, kind in shapes),
        scratch_shapes=scratch,
        input_output_aliases={} if alias is None else {alias: 0},
        compiler_params=limit(mebibytes),
        name=name,
    )(*[pltpu.with_memory_space_constraint(x, space) for x, space in operands])


def states_of(chunk, mine, keys, values, tie):
    pieces = HEADS // PIECE
    buf = pltpu.VMEM((pieces, keys.shape[0], WIDTH), jnp.bfloat16)
    return call(
        functools.partial(state_kernel, chunk, mine),
        "states",
        [(keys, pltpu.HBM), (values, pltpu.HBM)],
        [(pltpu.VMEM, (HEADS * E, E), jnp.float32)],
        [buf, buf, pltpu.SemaphoreType.DMA((2, pieces))],
        tie,
        mebibytes=6,
    )[0]


def vmem_call(kernel, name, shapes, tie, *arrays):
    return call(
        kernel,
        name,
        [(x, pltpu.VMEM) for x in arrays],
        [(pltpu.VMEM, shape, jnp.float32) for shape in shapes],
        tie=tie,
    )


def up_kernel(level, halve, keep_ref, got_ref, low_ref, *outs):
    keep, got = keep_ref[...], got_ref[...]
    low_ref[...] = jnp.where(bit_of(level) == 0, keep, got)
    total = keep + got
    if not halve:
        outs[0][...] = total
        return
    rows = total.shape[0] // 2
    one, two = total[:rows], total[rows:]
    lower = bit_of(level + 1) == 0
    outs[0][...] = jnp.where(lower, one, two)
    outs[1][...] = jnp.where(lower, two, one)


def go_up(level, halve, keep, got, tie):
    rows = keep.shape[0]
    shapes = [(rows, E)] + ([(rows // 2, E)] * 2 if halve else [(rows, E)])
    kernel = functools.partial(up_kernel, level, halve)
    return vmem_call(kernel, "up", shapes, tie, keep, got)


def group_kernel(bit, total_ref, got_ref, *refs):
    before_ref = refs[0] if len(refs) == 3 else None
    sum_ref, out_ref = refs[-2:]
    got = got_ref[...]
    before = jnp.where(bit_of(bit) == 0, 0.0, got)
    if before_ref is not None:
        before = before + before_ref[...]
    out_ref[...] = before
    sum_ref[...] = total_ref[...] + got


def go_along(bit, total, got, before, tie):
    arrays = [total, got] + ([] if before is None else [before])
    kernel = functools.partial(group_kernel, bit)
    return vmem_call(kernel, "group", [total.shape] * 2, tie, *arrays)


def split(level, before, low, own_ref, send_ref):
    lower = bit_of(level) == 0
    own_ref[...] = before + jnp.where(lower, 0.0, low)
    send_ref[...] = before + jnp.where(lower, low, 0.0)


def top_kernel(bit, level, got_ref, low_ref, *refs):
    own_ref, send_ref = refs[-2:]
    before = jnp.where(bit_of(bit) == 0, 0.0, got_ref[...])
    if len(refs) == 3:
        before = before + refs[0][...]
    split(level, before, low_ref[...], own_ref, send_ref)


def turn_down(bit, level, got, low, before, tie):
    arrays = [got, low] + ([] if before is None else [before])
    kernel = functools.partial(top_kernel, bit, level)
    return vmem_call(kernel, "top", [low.shape] * 2, tie, *arrays)


def down_kernel(level, own_ref, got_ref, low_ref, next_ref, send_ref):
    lower = bit_of(level + 1) == 0
    own, got = own_ref[...], got_ref[...]
    before = jnp.concatenate([jnp.where(lower, own, got), jnp.where(lower, got, own)], axis=0)
    split(level, before, low_ref[...], next_ref, send_ref)


def go_down(level, own, got, low, tie):
    kernel = functools.partial(down_kernel, level)
    return vmem_call(kernel, "down", [low.shape] * 2, tie, own, got, low)


def local_kernel(chunk, mine, q_ref, k_ref, v_ref, out_ref):
    rows = q_ref.shape[0]
    base = first_column(chunk, mine)
    causal = lax.broadcasted_iota(jnp.int32, (rows, rows), 0) >= lax.broadcasted_iota(
        jnp.int32, (rows, rows), 1
    )
    for h in range(HEADS):
        cols = lane_tile(base + h * E, E)
        scores = lax.dot_general(
            q_ref[:, cols],
            k_ref[:, cols],
            (((1,), (1,)), ((), ())),
            preferred_element_type=jnp.float32,
        )
        weights = jnp.where(causal, scores, 0.0).astype(jnp.bfloat16)
        out_ref[:, h * E : (h + 1) * E] = jnp.dot(
            weights, v_ref[:, cols], preferred_element_type=jnp.float32
        )


def local_mix(chunk, mine, queries, keys, values, tie):
    return call(
        functools.partial(local_kernel, chunk, mine),
        "local",
        [(queries, pltpu.VMEM), (keys, pltpu.VMEM), (values, pltpu.VMEM)],
        [(pltpu.VMEM, (queries.shape[0], HEADS * E), jnp.float32)],
        tie=tie,
        mebibytes=8,
    )[0]


def finish_kernel(chunk, mine, q_ref, m_ref, p_ref, gain_ref, *rest):
    out_ref, buf, sems = rest[-3:]
    base = first_column(chunk, mine)
    stores = []
    for piece in range(HEADS // PIECE):
        for h in range(PIECE):
            here = (piece * PIECE + h) * E
            cols = lane_tile(base + here, E)
            low = p_ref[here : here + E, :].astype(jnp.bfloat16)
            mixed = m_ref[:, here : here + E] + jnp.dot(
                q_ref[:, cols], low, preferred_element_type=jnp.float32
            )
            meansq = jnp.mean(mixed * mixed, axis=-1, keepdims=True)
            normed = mixed * lax.rsqrt(meansq + 1e-6) * gain_ref[:, cols]
            buf[piece, :, h * E : (h + 1) * E] = normed.astype(jnp.bfloat16)
        copy = pltpu.make_async_copy(
            buf.at[piece], out_ref.at[:, lane_tile(base + piece * WIDTH, WIDTH)], sems.at[piece]
        )
        copy.start()
        stores.append(copy)
    for copy in stores:
        copy.wait()


def finish(chunk, mine, queries, mixed, prefix, gain, out, tie):
    pieces = HEADS // PIECE
    arrays = [(queries, pltpu.VMEM), (mixed, pltpu.VMEM), (prefix, pltpu.VMEM), (gain, pltpu.VMEM)]
    if out is not None:
        arrays.append((out, pltpu.HBM))
    return call(
        functools.partial(finish_kernel, chunk, mine),
        "finish",
        arrays,
        [(pltpu.HBM, queries.shape, jnp.bfloat16)],
        [
            pltpu.VMEM((pieces, queries.shape[0], WIDTH), jnp.bfloat16),
            pltpu.SemaphoreType.DMA((pieces,)),
        ],
        tie,
        None if out is None else 4,
        mebibytes=6,
    )[0]


def shards(queries, keys, values, gain):
    groups, length = lax.axis_size("grp"), lax.axis_size("seq")
    devices = groups * length
    levels = length.bit_length() - 1
    group_bits = groups.bit_length() - 1
    gain = gain.reshape(1, H * E)
    chunks = range(CHUNKS)

    def swap(x, level):
        return lax.ppermute(x, AXES, [(i, i ^ (1 << level)) for i in range(devices)])

    latest = []

    def after(array, space=pltpu.VMEM):
        latest[:] = [(array, space)]
        return array

    todo = [(c, mine) for c in chunks for mine in (True, False)]
    mixed = {}

    def some_local():
        if todo:
            c, mine = todo.pop(0)
            mixed[c, mine] = after(local_mix(c, mine, queries, keys, values, latest))

    def up(level, c):
        halve = level < levels - 1
        low[c][level], keep[c], *send = go_up(level, halve, keep[c], got[c], latest)
        got[c] = swap(after(send[0] if halve else keep[c]), level + 1)

    keep, got = [None] * CHUNKS, [None] * CHUNKS
    low = [[None] * levels for _ in chunks]
    for c in chunks:
        got[c] = swap(after(states_of(c, False, keys, values, latest)), 0)
        keep[c] = after(states_of(c, True, keys, values, latest))
        up(0, c)
    some_local()
    for level in range(1, levels):
        for c in chunks:
            up(level, c)
        some_local()
    before = [None] * CHUNKS
    for bit in range(levels, levels + group_bits - 1):
        for c in chunks:
            keep[c], before[c] = go_along(bit, keep[c], got[c], before[c], latest)
            got[c] = swap(after(keep[c]), bit + 1)
        some_local()
    top, last_bit = levels - 1, levels + group_bits - 1
    for c in chunks:
        keep[c], send = turn_down(last_bit, top, got[c], low[c][top], before[c], latest)
        got[c] = swap(after(send), top)
    while todo:
        some_local()
    for level in range(top - 1, 0, -1):
        for c in chunks:
            keep[c], send = go_down(level, keep[c], got[c], low[c][level], latest)
            got[c] = swap(after(send), level)
    out = None
    for c in chunks:
        keep[c], send = go_down(0, keep[c], got[c], low[c][0], latest)
        got[c] = swap(after(send), 0)
        for mine, prefix in ((True, keep[c]), (False, got[c])):
            out = finish(c, mine, queries, mixed[c, mine], prefix, gain, out, latest)
            latest[:] = []
        after(out, pltpu.HBM)
    return out


def solution(mesh):
    rows = P(("grp", "seq"), None)
    return jax.shard_map(
        shards, mesh=mesh, in_specs=(rows, rows, rows, P()), out_specs=rows, check_vma=False
    )
```

```python
import functools

import jax
import jax.numpy as jnp
from jax import lax
from jax.experimental import pallas as pl
from jax.experimental.pallas import tpu as pltpu
from jax.sharding import PartitionSpec as P

H = 32
E = 128
AXES = ("grp", "seq")
HALF = H // 2
CHUNKS = 2
HEADS = HALF // CHUNKS
PIECE = 4
WIDTH = PIECE * E


def limit(mebibytes):
    return pltpu.CompilerParams(vmem_limit_bytes=mebibytes * 1024 * 1024)


def lane_tile(start, size):
    return pl.ds(pl.multiple_of(start, E), size)


def bit_of(level):
    index, length = lax.axis_index("seq"), lax.axis_size("seq")
    levels = length.bit_length() - 1
    if level < levels:
        return (index >> level) & 1
    return (lax.axis_index("grp") >> (level - levels)) & 1


def first_column(chunk, mine):
    core = bit_of(0)
    half = core if mine else 1 - core
    return (half * HALF + chunk * HEADS) * E


def state_kernel(chunk, mine, k_ref, v_ref, out_ref, k_buf, v_buf, sems):
    base = first_column(chunk, mine)
    copies = []
    for piece in range(HEADS // PIECE):
        for n, (ref, buf) in enumerate(((k_ref, k_buf), (v_ref, v_buf))):
            copy = pltpu.make_async_copy(
                ref.at[:, lane_tile(base + piece * WIDTH, WIDTH)],
                buf.at[piece],
                sems.at[n, piece],
            )
            copy.start()
            copies.append(copy)
    for piece in range(HEADS // PIECE):
        copies[2 * piece].wait()
        copies[2 * piece + 1].wait()
        for h in range(PIECE):
            cols = slice(h * E, (h + 1) * E)
            here = (piece * PIECE + h) * E
            out_ref[here : here + E, :] = lax.dot_general(
                k_buf[piece, :, cols],
                v_buf[piece, :, cols],
                (((0,), (0,)), ((), ())),
                preferred_element_type=jnp.float32,
            )


def call(kernel, name, arrays, shapes, scratch=(), tie=(), alias=None, mebibytes=4, flops=10**10):
    count, operands = len(arrays), list(arrays) + list(tie)

    def body(*refs):
        kernel(*refs[:count], *refs[len(operands) :])

    return pl.pallas_call(
        body,
        in_specs=[pl.BlockSpec(memory_space=space) for _, space in operands],
        out_specs=tuple(pl.BlockSpec(memory_space=space) for space, _, _ in shapes),
        out_shape=tuple(space(shape, kind) for space, shape, kind in shapes),
        scratch_shapes=scratch,
        input_output_aliases={} if alias is None else {alias: 0},
        compiler_params=limit(mebibytes),
        cost_estimate=pl.CostEstimate(flops=flops, bytes_accessed=1, transcendentals=0),
        name=name,
    )(*[pltpu.with_memory_space_constraint(x, space) for x, space in operands])


def states_of(chunk, mine, keys, values, tie):
    pieces = HEADS // PIECE
    buf = pltpu.VMEM((pieces, keys.shape[0], WIDTH), jnp.bfloat16)
    return call(
        functools.partial(state_kernel, chunk, mine),
        "states",
        [(keys, pltpu.HBM), (values, pltpu.HBM)],
        [(pltpu.VMEM, (HEADS * E, E), jnp.float32)],
        [buf, buf, pltpu.SemaphoreType.DMA((2, pieces))],
        tie,
        mebibytes=6,
    )[0]


def vmem_call(kernel, name, shapes, tie, *arrays):
    return call(
        kernel,
        name,
        [(x, pltpu.VMEM) for x in arrays],
        [(pltpu.VMEM, shape, jnp.float32) for shape in shapes],
        tie=tie,
    )


def up_kernel(level, halve, keep_ref, got_ref, low_ref, *outs):
    keep, got = keep_ref[...], got_ref[...]
    low_ref[...] = jnp.where(bit_of(level) == 0, keep, got)
    total = keep + got
    if not halve:
        outs[0][...] = total
        return
    rows = total.shape[0] // 2
    one, two = total[:rows], total[rows:]
    lower = bit_of(level + 1) == 0
    outs[0][...] = jnp.where(lower, one, two)
    outs[1][...] = jnp.where(lower, two, one)


def copy_kernel(x_ref, out_ref):
    out_ref[...] = x_ref[...]


def go_up(level, halve, keep, got, tie):
    rows = keep.shape[0]
    shapes = [(rows, E)] + ([(rows // 2, E)] * 2 if halve else [(rows, E)])
    kernel = functools.partial(up_kernel, level, halve)
    return vmem_call(kernel, "up", shapes, tie, keep, got)


def group_kernel(bit, other, turned, total_ref, got_ref, before_ref, send_ref):
    total, got = total_ref[...], got_ref[...]
    before = jnp.where(bit_of(bit) == 0, 0.0, got)
    before_ref[...] = before
    if turned:
        send_ref[...] = before + jnp.where(bit_of(other) == 0, total, 0.0)
    else:
        send_ref[...] = total + got


def go_along(bit, other, turned, total, got, tie):
    kernel = functools.partial(group_kernel, bit, other, turned)
    return vmem_call(kernel, "group", [total.shape] * 2, tie, total, got)


def split(level, before, low, own_ref, send_ref):
    lower = bit_of(level) == 0
    own_ref[...] = before + jnp.where(lower, 0.0, low)
    send_ref[...] = before + jnp.where(lower, low, 0.0)


def top_kernel(bit, turned, level, got_ref, low_ref, before_ref, own_ref, send_ref):
    got = got_ref[...]
    if not turned:
        got = jnp.where(bit_of(bit) == 0, 0.0, got)
    split(level, before_ref[...] + got, low_ref[...], own_ref, send_ref)


def turn_down(bit, turned, level, got, low, before, tie):
    kernel = functools.partial(top_kernel, bit, turned, level)
    return vmem_call(kernel, "top", [low.shape] * 2, tie, got, low, before)


def down_kernel(level, own_ref, got_ref, low_ref, next_ref, send_ref):
    lower = bit_of(level + 1) == 0
    own, got = own_ref[...], got_ref[...]
    before = jnp.concatenate([jnp.where(lower, own, got), jnp.where(lower, got, own)], axis=0)
    split(level, before, low_ref[...], next_ref, send_ref)


def go_down(level, own, got, low, tie):
    kernel = functools.partial(down_kernel, level)
    return vmem_call(kernel, "down", [low.shape] * 2, tie, own, got, low)


def local_kernel(chunk, mine, q_ref, k_ref, v_ref, out_ref, q_out_ref, k_buf, v_buf, sems):
    rows = q_ref.shape[0]
    base = first_column(chunk, mine)
    copies = []
    for piece in range(HEADS // PIECE):
        cols = lane_tile(base + piece * WIDTH, WIDTH)
        here = slice(piece * WIDTH, (piece + 1) * WIDTH)
        for n, (ref, buf) in enumerate(((q_ref, q_out_ref), (k_ref, k_buf), (v_ref, v_buf))):
            copy = pltpu.make_async_copy(ref.at[:, cols], buf.at[:, here], sems.at[n, piece])
            copy.start()
            copies.append(copy)
    causal = lax.broadcasted_iota(jnp.int32, (rows, rows), 0) >= lax.broadcasted_iota(
        jnp.int32, (rows, rows), 1
    )
    for h in range(HEADS):
        if h % PIECE == 0:
            for n in range(3):
                copies[h // PIECE * 3 + n].wait()
        cols = slice(h * E, (h + 1) * E)
        scores = lax.dot_general(
            q_out_ref[:, cols],
            k_buf[:, cols],
            (((1,), (1,)), ((), ())),
            preferred_element_type=jnp.float32,
        )
        weights = jnp.where(causal, scores, 0.0).astype(jnp.bfloat16)
        out_ref[:, cols] = jnp.dot(weights, v_buf[:, cols], preferred_element_type=jnp.float32)


def local_mix(chunk, mine, queries, keys, values, tie):
    shape = (queries.shape[0], HEADS * E)
    buf = pltpu.VMEM(shape, jnp.bfloat16)
    return call(
        functools.partial(local_kernel, chunk, mine),
        "local",
        [(queries, pltpu.HBM), (keys, pltpu.HBM), (values, pltpu.HBM)],
        [(pltpu.VMEM, shape, jnp.float32), (pltpu.VMEM, shape, jnp.bfloat16)],
        [buf, buf, pltpu.SemaphoreType.DMA((3, HEADS // PIECE))],
        tie,
        mebibytes=10,
    )


def finish_kernel(chunk, mine, q_ref, m_ref, p_ref, gain_ref, *rest):
    out_ref, buf, sems = rest[-3:]
    base = first_column(chunk, mine)
    stores = []
    for piece in range(HEADS // PIECE):
        for h in range(PIECE):
            here = (piece * PIECE + h) * E
            cols = lane_tile(base + here, E)
            low = p_ref[here : here + E, :].astype(jnp.bfloat16)
            mixed = m_ref[:, here : here + E] + jnp.dot(
                q_ref[:, here : here + E], low, preferred_element_type=jnp.float32
            )
            meansq = jnp.mean(mixed * mixed, axis=-1, keepdims=True)
            normed = mixed * lax.rsqrt(meansq + 1e-6) * gain_ref[:, cols]
            buf[piece, :, h * E : (h + 1) * E] = normed.astype(jnp.bfloat16)
        copy = pltpu.make_async_copy(
            buf.at[piece], out_ref.at[:, lane_tile(base + piece * WIDTH, WIDTH)], sems.at[piece]
        )
        copy.start()
        stores.append(copy)
    for copy in stores:
        copy.wait()


def finish(chunk, mine, shape, mixed, queries, prefix, gain, out, tie):
    pieces = HEADS // PIECE
    arrays = [(queries, pltpu.VMEM), (mixed, pltpu.VMEM), (prefix, pltpu.VMEM), (gain, pltpu.VMEM)]
    if out is not None:
        arrays.append((out, pltpu.HBM))
    return call(
        functools.partial(finish_kernel, chunk, mine),
        "finish",
        arrays,
        [(pltpu.HBM, shape, jnp.bfloat16)],
        [
            pltpu.VMEM((pieces, shape[0], WIDTH), jnp.bfloat16),
            pltpu.SemaphoreType.DMA((pieces,)),
        ],
        tie,
        None if out is None else 4,
        mebibytes=6,
    )[0]


def shards(queries, keys, values, gain):
    groups, length = lax.axis_size("grp"), lax.axis_size("seq")
    devices = groups * length
    levels = length.bit_length() - 1
    gain = gain.reshape(1, H * E)
    chunks = range(CHUNKS)

    def swap(x, level):
        return lax.ppermute(x, AXES, [(i, i ^ (1 << level)) for i in range(devices)])

    latest = []

    def after(array, space=pltpu.VMEM):
        latest[:] = [(array, space)]
        return array

    todo = [(c, mine) for c in chunks for mine in (True, False)]
    mixed = {}

    def some_local():
        if todo:
            c, mine = todo.pop(0)
            mixed[c, mine] = local_mix(c, mine, queries, keys, values, latest)
            after(mixed[c, mine][0])

    order = [(levels, levels + 1), (levels + 1, levels)]

    def up(level, c):
        halve = level < levels - 1
        low[c][level], keep[c], *send = go_up(level, halve, keep[c], got[c], latest)
        along = level + 1 if halve else order[c % 2][0]
        got[c] = swap(after(send[0] if halve else keep[c]), along)

    keep, got, before = [None] * CHUNKS, [None] * CHUNKS, [None] * CHUNKS
    low = [[None] * levels for _ in chunks]
    for c in chunks:
        got[c] = swap(after(states_of(c, False, keys, values, latest)), 0)
        keep[c] = after(states_of(c, True, keys, values, latest))
        up(0, c)
    some_local()
    for level in range(1, levels):
        for c in chunks:
            up(level, c)
            if level == 1:
                some_local()
    for c in chunks:
        bit, other = order[c % 2]
        before[c], send = go_along(bit, other, c % 2 == 1, keep[c], got[c], latest)
        got[c] = swap(after(send), other)
    top = levels - 1
    for c in chunks:
        turned = c % 2 == 1
        keep[c], send = turn_down(order[0][1], turned, top, got[c], low[c][top], before[c], latest)
        got[c] = swap(after(send), top)
    while todo:
        some_local()
    gain = after(vmem_call(copy_kernel, "gain", [gain.shape], latest, gain)[0])
    for level in range(top - 1, 0, -1):
        for c in chunks:
            keep[c], send = go_down(level, keep[c], got[c], low[c][level], latest)
            got[c] = swap(after(send), level)
    out = None
    for c in chunks:
        keep[c], send = go_down(0, keep[c], got[c], low[c][0], latest)
        got[c] = swap(after(send), 0)
        for mine, prefix in ((True, keep[c]), (False, got[c])):
            out = finish(c, mine, queries.shape, *mixed[c, mine], prefix, gain, out, latest)
            latest[:] = []
        after(out, pltpu.HBM)
    return out


def solution(mesh):
    rows = P(("grp", "seq"), None)
    return jax.shard_map(
        shards, mesh=mesh, in_specs=(rows, rows, rows, P()), out_specs=rows, check_vma=False
    )
```

```python
import functools

import jax
import jax.numpy as jnp
from jax import lax
from jax.experimental import pallas as pl
from jax.experimental.pallas import tpu as pltpu
from jax.sharding import PartitionSpec as P

H = 32
E = 128
AXES = ("grp", "seq")
HALF = H // 2
CHUNKS = 2
HEADS = HALF // CHUNKS
PIECE = 4
HINT = 7 * 10**9
WIDTH = PIECE * E


def limit(mebibytes):
    return pltpu.CompilerParams(vmem_limit_bytes=mebibytes * 1024 * 1024)


def lane_tile(start, size):
    return pl.ds(pl.multiple_of(start, E), size)


def bit_of(level):
    index, length = lax.axis_index("seq"), lax.axis_size("seq")
    levels = length.bit_length() - 1
    if level < levels:
        return (index >> level) & 1
    return (lax.axis_index("grp") >> (level - levels)) & 1


def first_column(chunk, mine):
    core = bit_of(0)
    half = core if mine else 1 - core
    return (half * HALF + chunk * HEADS) * E


def state_kernel(chunk, mine, k_ref, v_ref, out_ref, k_buf, v_buf, sems):
    base = first_column(chunk, mine)
    copies = []
    for piece in range(HEADS // PIECE):
        for n, (ref, buf) in enumerate(((k_ref, k_buf), (v_ref, v_buf))):
            copy = pltpu.make_async_copy(
                ref.at[:, lane_tile(base + piece * WIDTH, WIDTH)],
                buf.at[piece],
                sems.at[n, piece],
            )
            copy.start()
            copies.append(copy)
    for piece in range(HEADS // PIECE):
        copies[2 * piece].wait()
        copies[2 * piece + 1].wait()
        for h in range(PIECE):
            cols = slice(h * E, (h + 1) * E)
            here = (piece * PIECE + h) * E
            out_ref[here : here + E, :] = lax.dot_general(
                k_buf[piece, :, cols],
                v_buf[piece, :, cols],
                (((0,), (0,)), ((), ())),
                preferred_element_type=jnp.float32,
            )


def call(kernel, name, arrays, shapes, scratch=(), tie=(), alias=None, mebibytes=4):
    count, operands = len(arrays), list(arrays) + list(tie)

    def body(*refs):
        kernel(*refs[:count], *refs[len(operands) :])

    return pl.pallas_call(
        body,
        in_specs=[pl.BlockSpec(memory_space=space) for _, space in operands],
        out_specs=tuple(pl.BlockSpec(memory_space=space) for space, _, _ in shapes),
        out_shape=tuple(space(shape, kind) for space, shape, kind in shapes),
        scratch_shapes=scratch,
        input_output_aliases={} if alias is None else {alias: 0},
        compiler_params=limit(mebibytes),
        cost_estimate=pl.CostEstimate(flops=HINT, bytes_accessed=1, transcendentals=0),
        name=name,
    )(*[pltpu.with_memory_space_constraint(x, space) for x, space in operands])


def states_of(chunk, mine, keys, values, tie):
    pieces = HEADS // PIECE
    buf = pltpu.VMEM((pieces, keys.shape[0], WIDTH), jnp.bfloat16)
    return call(
        functools.partial(state_kernel, chunk, mine),
        "states",
        [(keys, pltpu.HBM), (values, pltpu.HBM)],
        [(pltpu.VMEM, (HEADS * E, E), jnp.float32)],
        [buf, buf, pltpu.SemaphoreType.DMA((2, pieces))],
        tie,
        mebibytes=6,
    )[0]


def vmem_call(kernel, name, shapes, tie, *arrays):
    return call(
        kernel,
        name,
        [(x, pltpu.VMEM) for x in arrays],
        [(pltpu.VMEM, shape, jnp.float32) for shape in shapes],
        tie=tie,
    )


def up_kernel(level, halve, keep_ref, got_ref, low_ref, *outs):
    keep, got = keep_ref[...], got_ref[...]
    low_ref[...] = jnp.where(bit_of(level) == 0, keep, got)
    total = keep + got
    if not halve:
        outs[0][...] = total
        return
    rows = total.shape[0] // 2
    one, two = total[:rows], total[rows:]
    lower = bit_of(level + 1) == 0
    outs[0][...] = jnp.where(lower, one, two)
    outs[1][...] = jnp.where(lower, two, one)


def pick(lower, one, two):
    return jnp.where(lower, one, two), jnp.where(lower, two, one)


def first_kernel(keep_ref, got_ref, low_ref, *outs):
    keep, got = keep_ref[...], got_ref[...]
    low_ref[...] = jnp.where(bit_of(0) == 0, keep, got)
    total = keep + got
    rows = total.shape[0] // 2
    mine, other = pick(bit_of(1) == 0, total[:rows], total[rows:])
    for n, half in enumerate((other, mine)):
        stays, goes_on = pick(bit_of(2) == 0, half[: rows // 2], half[rows // 2 :])
        outs[2 * n][...] = goes_on
        outs[2 * n + 1][...] = stays


def first_up(keep, got, tie):
    rows = keep.shape[0]
    shapes = [(rows, E)] + [(rows // 4, E)] * 4
    return vmem_call(first_kernel, "first_up", shapes, tie, keep, got)


def part_kernel(before_ref, low_ref, own_ref, send_ref):
    split(1, before_ref[...], low_ref[...], own_ref, send_ref)


def part_down(before, low, tie):
    return vmem_call(part_kernel, "part", [low.shape] * 2, tie, before, low)


def last_kernel(own_ref, own_on_ref, got_ref, got_on_ref, low_ref, next_ref, send_ref):
    lower = bit_of(2) == 0
    mine = jnp.concatenate(pick(lower, own_ref[...], own_on_ref[...]), axis=0)
    other = jnp.concatenate(pick(lower, got_ref[...], got_on_ref[...]), axis=0)
    before = jnp.concatenate(pick(bit_of(1) == 0, mine, other), axis=0)
    split(0, before, low_ref[...], next_ref, send_ref)


def last_down(own, got, low, tie):
    return vmem_call(last_kernel, "last_down", [low.shape] * 2, tie, *own, *got, low)


def copy_kernel(x_ref, out_ref):
    out_ref[...] = x_ref[...]


def go_up(level, halve, keep, got, tie):
    rows = keep.shape[0]
    shapes = [(rows, E)] + ([(rows // 2, E)] * 2 if halve else [(rows, E)])
    kernel = functools.partial(up_kernel, level, halve)
    return vmem_call(kernel, "up", shapes, tie, keep, got)


def group_kernel(bit, other, turned, total_ref, got_ref, before_ref, send_ref):
    total, got = total_ref[...], got_ref[...]
    before = jnp.where(bit_of(bit) == 0, 0.0, got)
    before_ref[...] = before
    if turned:
        send_ref[...] = before + jnp.where(bit_of(other) == 0, total, 0.0)
    else:
        send_ref[...] = total + got


def go_along(bit, other, turned, total, got, tie):
    kernel = functools.partial(group_kernel, bit, other, turned)
    return vmem_call(kernel, "group", [total.shape] * 2, tie, total, got)


def split(level, before, low, own_ref, send_ref):
    lower = bit_of(level) == 0
    own_ref[...] = before + jnp.where(lower, 0.0, low)
    send_ref[...] = before + jnp.where(lower, low, 0.0)


def top_kernel(bit, turned, level, got_ref, low_ref, before_ref, own_ref, send_ref):
    got = got_ref[...]
    if not turned:
        got = jnp.where(bit_of(bit) == 0, 0.0, got)
    split(level, before_ref[...] + got, low_ref[...], own_ref, send_ref)


def turn_down(bit, turned, level, got, low, before, tie):
    kernel = functools.partial(top_kernel, bit, turned, level)
    return vmem_call(kernel, "top", [low.shape] * 2, tie, got, low, before)


def down_kernel(level, own_ref, got_ref, low_ref, next_ref, send_ref):
    lower = bit_of(level + 1) == 0
    own, got = own_ref[...], got_ref[...]
    before = jnp.concatenate([jnp.where(lower, own, got), jnp.where(lower, got, own)], axis=0)
    split(level, before, low_ref[...], next_ref, send_ref)


def go_down(level, own, got, low, tie):
    kernel = functools.partial(down_kernel, level)
    return vmem_call(kernel, "down", [low.shape] * 2, tie, own, got, low)


def local_kernel(chunk, mine, q_ref, k_ref, v_ref, out_ref, q_out_ref, k_buf, v_buf, sems):
    rows = q_ref.shape[0]
    base = first_column(chunk, mine)
    copies = []
    for piece in range(HEADS // PIECE):
        cols = lane_tile(base + piece * WIDTH, WIDTH)
        here = slice(piece * WIDTH, (piece + 1) * WIDTH)
        for n, (ref, buf) in enumerate(((q_ref, q_out_ref), (k_ref, k_buf), (v_ref, v_buf))):
            copy = pltpu.make_async_copy(ref.at[:, cols], buf.at[:, here], sems.at[n, piece])
            copy.start()
            copies.append(copy)
    causal = lax.broadcasted_iota(jnp.int32, (rows, rows), 0) >= lax.broadcasted_iota(
        jnp.int32, (rows, rows), 1
    )
    for h in range(HEADS):
        if h % PIECE == 0:
            for n in range(3):
                copies[h // PIECE * 3 + n].wait()
        cols = slice(h * E, (h + 1) * E)
        scores = lax.dot_general(
            q_out_ref[:, cols],
            k_buf[:, cols],
            (((1,), (1,)), ((), ())),
            preferred_element_type=jnp.float32,
        )
        weights = jnp.where(causal, scores, 0.0).astype(jnp.bfloat16)
        out_ref[:, cols] = jnp.dot(weights, v_buf[:, cols], preferred_element_type=jnp.float32)


def local_mix(chunk, mine, queries, keys, values, tie):
    shape = (queries.shape[0], HEADS * E)
    buf = pltpu.VMEM(shape, jnp.bfloat16)
    return call(
        functools.partial(local_kernel, chunk, mine),
        "local",
        [(queries, pltpu.HBM), (keys, pltpu.HBM), (values, pltpu.HBM)],
        [(pltpu.VMEM, shape, jnp.float32), (pltpu.VMEM, shape, jnp.bfloat16)],
        [buf, buf, pltpu.SemaphoreType.DMA((3, HEADS // PIECE))],
        tie,
        mebibytes=10,
    )


def finish_kernel(chunk, mine, q_ref, m_ref, p_ref, gain_ref, *rest):
    out_ref, buf, sems = rest[-3:]
    base = first_column(chunk, mine)
    stores = []
    for piece in range(HEADS // PIECE):
        for h in range(PIECE):
            here = (piece * PIECE + h) * E
            cols = lane_tile(base + here, E)
            low = p_ref[here : here + E, :].astype(jnp.bfloat16)
            mixed = m_ref[:, here : here + E] + jnp.dot(
                q_ref[:, here : here + E], low, preferred_element_type=jnp.float32
            )
            meansq = jnp.mean(mixed * mixed, axis=-1, keepdims=True)
            normed = mixed * lax.rsqrt(meansq + 1e-6) * gain_ref[:, cols]
            buf[piece, :, h * E : (h + 1) * E] = normed.astype(jnp.bfloat16)
        copy = pltpu.make_async_copy(
            buf.at[piece], out_ref.at[:, lane_tile(base + piece * WIDTH, WIDTH)], sems.at[piece]
        )
        copy.start()
        stores.append(copy)
    for copy in stores:
        copy.wait()


def finish(chunk, mine, shape, mixed, queries, prefix, gain, out, tie):
    pieces = HEADS // PIECE
    arrays = [(queries, pltpu.VMEM), (mixed, pltpu.VMEM), (prefix, pltpu.VMEM), (gain, pltpu.VMEM)]
    if out is not None:
        arrays.append((out, pltpu.HBM))
    return call(
        functools.partial(finish_kernel, chunk, mine),
        "finish",
        arrays,
        [(pltpu.HBM, shape, jnp.bfloat16)],
        [
            pltpu.VMEM((pieces, shape[0], WIDTH), jnp.bfloat16),
            pltpu.SemaphoreType.DMA((pieces,)),
        ],
        tie,
        None if out is None else 4,
        mebibytes=6,
    )[0]


def shards(queries, keys, values, gain):
    groups, length = lax.axis_size("grp"), lax.axis_size("seq")
    devices = groups * length
    levels = length.bit_length() - 1
    gain = gain.reshape(1, H * E)
    chunks = range(CHUNKS)

    def swap(x, level):
        return lax.ppermute(x, AXES, [(i, i ^ (1 << level)) for i in range(devices)])

    latest = []

    def after(array, space=pltpu.VMEM):
        latest[:] = [(array, space)]
        return array

    todo = [(c, mine) for c in chunks for mine in (True, False)]
    mixed = {}

    def some_local():
        if todo:
            c, mine = todo.pop(0)
            mixed[c, mine] = local_mix(c, mine, queries, keys, values, latest)
            after(mixed[c, mine][0])

    order = [(levels, levels + 1), (levels + 1, levels)]

    def up(level, c):
        halve = level < levels - 1
        low[c][level], keep[c], *send = go_up(level, halve, keep[c], got[c], latest)
        along = level + 1 if halve else order[c % 2][0]
        got[c] = swap(after(send[0] if halve else keep[c]), along)

    keep, got, before = [None] * CHUNKS, [None] * CHUNKS, [None] * CHUNKS
    low = [[None] * levels for _ in chunks]
    part_keep, part_got, part_low = ([[None, None] for _ in chunks] for _ in range(3))
    for c in chunks:
        got[c] = swap(after(states_of(c, False, keys, values, latest)), 0)
        keep[c] = after(states_of(c, True, keys, values, latest))
        low[c][0], send_on, send, part_keep[c][1], part_keep[c][0] = first_up(keep[c], got[c], latest)
        part_got[c][1] = swap(after(send_on), 1)
        part_got[c][0] = swap(send, 1)
    some_local()
    for c in chunks:
        part_low[c][1], send = go_up(1, False, part_keep[c][1], part_got[c][1], latest)
        got[c] = swap(after(send), 2)
        part_low[c][0], keep[c] = go_up(1, False, part_keep[c][0], part_got[c][0], latest)
        after(keep[c])
        some_local()
    for level in range(2, levels):
        for c in chunks:
            up(level, c)
    for c in chunks:
        bit, other = order[c % 2]
        before[c], send = go_along(bit, other, c % 2 == 1, keep[c], got[c], latest)
        got[c] = swap(after(send), other)
    top = levels - 1
    def part(c, n, before):
        part_keep[c][n], send = part_down(before, part_low[c][n], latest)
        part_got[c][n] = swap(after(send), 1)

    for c in chunks:
        turned = c % 2 == 1
        keep[c], send = turn_down(order[0][1], turned, top, got[c], low[c][top], before[c], latest)
        got[c] = swap(after(send), top)
        if top == 2:
            part(c, 0, keep[c])
    while todo:
        some_local()
    gain = after(vmem_call(copy_kernel, "gain", [gain.shape], latest, gain)[0])
    for level in range(top - 1, 1, -1):
        for c in chunks:
            keep[c], send = go_down(level, keep[c], got[c], low[c][level], latest)
            got[c] = swap(after(send), level)
            if level == 2:
                part(c, 0, keep[c])
    for c in chunks:
        part(c, 1, got[c])
    out = None
    for c in chunks:
        keep[c], send = last_down(part_keep[c], part_got[c], low[c][0], latest)
        got[c] = swap(after(send), 0)
        for mine, prefix in ((True, keep[c]), (False, got[c])):
            out = finish(c, mine, queries.shape, *mixed[c, mine], prefix, gain, out, latest)
            latest[:] = []
        after(out, pltpu.HBM)
    return out


def solution(mesh):
    rows = P(("grp", "seq"), None)
    return jax.shard_map(
        shards, mesh=mesh, in_specs=(rows, rows, rows, P()), out_specs=rows, check_vma=False
    )
```

```python
import functools

import jax
import jax.numpy as jnp
from jax import lax
from jax.experimental import pallas as pl
from jax.experimental.pallas import tpu as pltpu
from jax.sharding import PartitionSpec as P

H = 32
E = 128
AXES = ("grp", "seq")
HALF = H // 2
CHUNKS = 2
HEADS = HALF // CHUNKS
PIECE = 4
HINT = 7 * 10**9
WIDTH = PIECE * E


def limit(mebibytes):
    return pltpu.CompilerParams(vmem_limit_bytes=mebibytes * 1024 * 1024)


def lane_tile(start, size):
    return pl.ds(pl.multiple_of(start, E), size)


def bit_of(level):
    index, length = lax.axis_index("seq"), lax.axis_size("seq")
    levels = length.bit_length() - 1
    if level < levels:
        return (index >> level) & 1
    return (lax.axis_index("grp") >> (level - levels)) & 1


def first_column(chunk, mine):
    core = bit_of(0)
    half = core if mine else 1 - core
    return (half * HALF + chunk * HEADS) * E


def load_columns(base, refs, bufs, sems):
    copies = []
    for piece in range(HEADS // PIECE):
        cols = lane_tile(base + piece * WIDTH, WIDTH)
        here = slice(piece * WIDTH, (piece + 1) * WIDTH)
        copies.append(
            [
                pltpu.make_async_copy(ref.at[:, cols], buf.at[:, here], sems.at[n, piece])
                for n, (ref, buf) in enumerate(zip(refs, bufs))
            ]
        )
        for copy in copies[-1]:
            copy.start()
    return copies


def state_kernel(chunk, mine, k_ref, v_ref, out_ref, k_out_ref, v_out_ref, sems):
    base = first_column(chunk, mine)
    copies = load_columns(base, (k_ref, v_ref), (k_out_ref, v_out_ref), sems)
    for h in range(HEADS):
        if h % PIECE == 0:
            for copy in copies[h // PIECE]:
                copy.wait()
        cols = slice(h * E, (h + 1) * E)
        out_ref[cols, :] = lax.dot_general(
            k_out_ref[:, cols],
            v_out_ref[:, cols],
            (((0,), (0,)), ((), ())),
            preferred_element_type=jnp.float32,
        )


def call(kernel, name, arrays, shapes, scratch=(), tie=(), alias=None, mebibytes=4):
    count, operands = len(arrays), list(arrays) + list(tie)

    def body(*refs):
        kernel(*refs[:count], *refs[len(operands) :])

    return pl.pallas_call(
        body,
        in_specs=[pl.BlockSpec(memory_space=space) for _, space in operands],
        out_specs=tuple(pl.BlockSpec(memory_space=space) for space, _, _ in shapes),
        out_shape=tuple(space(shape, kind) for space, shape, kind in shapes),
        scratch_shapes=scratch,
        input_output_aliases={} if alias is None else {alias: 0},
        compiler_params=limit(mebibytes),
        cost_estimate=pl.CostEstimate(flops=HINT, bytes_accessed=1, transcendentals=0),
        name=name,
    )(*[pltpu.with_memory_space_constraint(x, space) for x, space in operands])


def states_of(chunk, mine, keys, values, tie):
    columns = (pltpu.VMEM, (keys.shape[0], HEADS * E), jnp.bfloat16)
    return call(
        functools.partial(state_kernel, chunk, mine),
        "states",
        [(keys, pltpu.HBM), (values, pltpu.HBM)],
        [(pltpu.VMEM, (HEADS * E, E), jnp.float32), columns, columns],
        [pltpu.SemaphoreType.DMA((2, HEADS // PIECE))],
        tie,
        mebibytes=6,
    )


def vmem_call(kernel, name, shapes, tie, *arrays):
    return call(
        kernel,
        name,
        [(x, pltpu.VMEM) for x in arrays],
        [(pltpu.VMEM, shape, jnp.float32) for shape in shapes],
        tie=tie,
    )


def up_kernel(level, halve, keep_ref, got_ref, low_ref, *outs):
    keep, got = keep_ref[...], got_ref[...]
    low_ref[...] = jnp.where(bit_of(level) == 0, keep, got)
    total = keep + got
    if not halve:
        outs[0][...] = total
        return
    rows = total.shape[0] // 2
    one, two = total[:rows], total[rows:]
    lower = bit_of(level + 1) == 0
    outs[0][...] = jnp.where(lower, one, two)
    outs[1][...] = jnp.where(lower, two, one)


def pick(lower, one, two):
    return jnp.where(lower, one, two), jnp.where(lower, two, one)


def first_kernel(keep_ref, got_ref, low_ref, *outs):
    keep, got = keep_ref[...], got_ref[...]
    low_ref[...] = jnp.where(bit_of(0) == 0, keep, got)
    total = keep + got
    rows = total.shape[0] // 2
    mine, other = pick(bit_of(1) == 0, total[:rows], total[rows:])
    for n, half in enumerate((other, mine)):
        stays, goes_on = pick(bit_of(2) == 0, half[: rows // 2], half[rows // 2 :])
        outs[2 * n][...] = goes_on
        outs[2 * n + 1][...] = stays


def first_up(keep, got, tie):
    rows = keep.shape[0]
    shapes = [(rows, E)] + [(rows // 4, E)] * 4
    return vmem_call(first_kernel, "first_up", shapes, tie, keep, got)


def part_kernel(before_ref, low_ref, own_ref, send_ref):
    split(1, before_ref[...], low_ref[...], own_ref, send_ref)


def part_down(before, low, tie):
    return vmem_call(part_kernel, "part", [low.shape] * 2, tie, before, low)


def last_kernel(own_ref, own_on_ref, got_ref, got_on_ref, low_ref, next_ref, send_ref):
    lower = bit_of(2) == 0
    mine = jnp.concatenate(pick(lower, own_ref[...], own_on_ref[...]), axis=0)
    other = jnp.concatenate(pick(lower, got_ref[...], got_on_ref[...]), axis=0)
    before = jnp.concatenate(pick(bit_of(1) == 0, mine, other), axis=0)
    split(0, before, low_ref[...], next_ref, send_ref)


def last_down(own, got, low, tie):
    return vmem_call(last_kernel, "last_down", [low.shape] * 2, tie, *own, *got, low)


def copy_kernel(x_ref, out_ref):
    out_ref[...] = x_ref[...]


def go_up(level, halve, keep, got, tie):
    rows = keep.shape[0]
    shapes = [(rows, E)] + ([(rows // 2, E)] * 2 if halve else [(rows, E)])
    kernel = functools.partial(up_kernel, level, halve)
    return vmem_call(kernel, "up", shapes, tie, keep, got)


def group_kernel(bit, other, turned, total_ref, got_ref, before_ref, send_ref):
    total, got = total_ref[...], got_ref[...]
    before = jnp.where(bit_of(bit) == 0, 0.0, got)
    before_ref[...] = before
    if turned:
        send_ref[...] = before + jnp.where(bit_of(other) == 0, total, 0.0)
    else:
        send_ref[...] = total + got


def go_along(bit, other, turned, total, got, tie):
    kernel = functools.partial(group_kernel, bit, other, turned)
    return vmem_call(kernel, "group", [total.shape] * 2, tie, total, got)


def split(level, before, low, own_ref, send_ref):
    lower = bit_of(level) == 0
    own_ref[...] = before + jnp.where(lower, 0.0, low)
    send_ref[...] = before + jnp.where(lower, low, 0.0)


def top_kernel(bit, turned, level, got_ref, low_ref, before_ref, own_ref, send_ref):
    got = got_ref[...]
    if not turned:
        got = jnp.where(bit_of(bit) == 0, 0.0, got)
    split(level, before_ref[...] + got, low_ref[...], own_ref, send_ref)


def turn_down(bit, turned, level, got, low, before, tie):
    kernel = functools.partial(top_kernel, bit, turned, level)
    return vmem_call(kernel, "top", [low.shape] * 2, tie, got, low, before)


def down_kernel(level, own_ref, got_ref, low_ref, next_ref, send_ref):
    lower = bit_of(level + 1) == 0
    own, got = own_ref[...], got_ref[...]
    before = jnp.concatenate([jnp.where(lower, own, got), jnp.where(lower, got, own)], axis=0)
    split(level, before, low_ref[...], next_ref, send_ref)


def go_down(level, own, got, low, tie):
    kernel = functools.partial(down_kernel, level)
    return vmem_call(kernel, "down", [low.shape] * 2, tie, own, got, low)


def local_kernel(chunk, mine, q_ref, k_ref, v_ref, out_ref):
    rows = k_ref.shape[0]
    base = first_column(chunk, mine)
    causal = lax.broadcasted_iota(jnp.int32, (rows, rows), 0) >= lax.broadcasted_iota(
        jnp.int32, (rows, rows), 1
    )
    for h in range(HEADS):
        cols = slice(h * E, (h + 1) * E)
        scores = lax.dot_general(
            q_ref[:, lane_tile(base + h * E, E)],
            k_ref[:, cols],
            (((1,), (1,)), ((), ())),
            preferred_element_type=jnp.float32,
        )
        weights = jnp.where(causal, scores, 0.0).astype(jnp.bfloat16)
        out_ref[:, cols] = jnp.dot(weights, v_ref[:, cols], preferred_element_type=jnp.float32)


def local_mix(chunk, mine, queries, keys, values, tie):
    return call(
        functools.partial(local_kernel, chunk, mine),
        "local",
        [(queries, pltpu.VMEM), (keys, pltpu.VMEM), (values, pltpu.VMEM)],
        [(pltpu.VMEM, keys.shape, jnp.float32)],
        tie=tie,
        mebibytes=8,
    )[0]


def finish_kernel(chunk, mine, q_ref, m_ref, p_ref, gain_ref, *rest):
    out_ref, buf, sems = rest[-3:]
    base = first_column(chunk, mine)
    stores = []
    for piece in range(HEADS // PIECE):
        for h in range(PIECE):
            here = (piece * PIECE + h) * E
            cols = lane_tile(base + here, E)
            low = p_ref[here : here + E, :].astype(jnp.bfloat16)
            mixed = m_ref[:, here : here + E] + jnp.dot(
                q_ref[:, cols], low, preferred_element_type=jnp.float32
            )
            meansq = jnp.mean(mixed * mixed, axis=-1, keepdims=True)
            normed = mixed * lax.rsqrt(meansq + 1e-6) * gain_ref[:, cols]
            buf[piece, :, h * E : (h + 1) * E] = normed.astype(jnp.bfloat16)
        copy = pltpu.make_async_copy(
            buf.at[piece], out_ref.at[:, lane_tile(base + piece * WIDTH, WIDTH)], sems.at[piece]
        )
        copy.start()
        stores.append(copy)
    for copy in stores:
        copy.wait()


def finish(chunk, mine, shape, mixed, queries, prefix, gain, out, tie):
    pieces = HEADS // PIECE
    arrays = [(queries, pltpu.VMEM), (mixed, pltpu.VMEM), (prefix, pltpu.VMEM), (gain, pltpu.VMEM)]
    if out is not None:
        arrays.append((out, pltpu.HBM))
    return call(
        functools.partial(finish_kernel, chunk, mine),
        "finish",
        arrays,
        [(pltpu.HBM, shape, jnp.bfloat16)],
        [
            pltpu.VMEM((pieces, shape[0], WIDTH), jnp.bfloat16),
            pltpu.SemaphoreType.DMA((pieces,)),
        ],
        tie,
        None if out is None else 4,
        mebibytes=6,
    )[0]


def shards(queries, keys, values, gain):
    groups, length = lax.axis_size("grp"), lax.axis_size("seq")
    devices = groups * length
    levels = length.bit_length() - 1
    gain = gain.reshape(1, H * E)
    chunks = range(CHUNKS)

    def swap(x, level):
        return lax.ppermute(x, AXES, [(i, i ^ (1 << level)) for i in range(devices)])

    latest = []

    def after(array, space=pltpu.VMEM):
        latest[:] = [(array, space)]
        return array

    todo = [(c, mine) for c in chunks for mine in (True, False)]
    mixed, columns = {}, {}

    def some_local():
        if todo:
            this = todo.pop(0)
            mixed[this] = after(local_mix(*this, queries, *columns[this], latest))

    order = [(levels, levels + 1), (levels + 1, levels)]

    def up(level, c):
        halve = level < levels - 1
        low[c][level], keep[c], *send = go_up(level, halve, keep[c], got[c], latest)
        along = level + 1 if halve else order[c % 2][0]
        got[c] = swap(after(send[0] if halve else keep[c]), along)

    keep, got, before = [None] * CHUNKS, [None] * CHUNKS, [None] * CHUNKS
    low = [[None] * levels for _ in chunks]
    part_keep, part_got, part_low = ([[None, None] for _ in chunks] for _ in range(3))
    for c in chunks:
        send, *columns[c, False] = states_of(c, False, keys, values, latest)
        got[c] = swap(after(send), 0)
        keep[c], *columns[c, True] = states_of(c, True, keys, values, latest)
        after(keep[c])
        low[c][0], send_on, send, part_keep[c][1], part_keep[c][0] = first_up(keep[c], got[c], latest)
        part_got[c][1] = swap(after(send_on), 1)
        part_got[c][0] = swap(send, 1)
    for c in chunks:
        part_low[c][1], send = go_up(1, False, part_keep[c][1], part_got[c][1], latest)
        got[c] = swap(after(send), 2)
        part_low[c][0], keep[c] = go_up(1, False, part_keep[c][0], part_got[c][0], latest)
        after(keep[c])
        some_local()
    for level in range(2, levels):
        for c in chunks:
            up(level, c)
            if level == levels - 1 and c == 0:
                some_local()
    for c in chunks:
        bit, other = order[c % 2]
        before[c], send = go_along(bit, other, c % 2 == 1, keep[c], got[c], latest)
        got[c] = swap(after(send), other)
        if c == 0:
            while todo:
                some_local()
            gain = after(vmem_call(copy_kernel, "gain", [gain.shape], latest, gain)[0])
    top = levels - 1
    def part(c, n, before):
        part_keep[c][n], send = part_down(before, part_low[c][n], latest)
        part_got[c][n] = swap(after(send), 1)

    for c in chunks:
        turned = c % 2 == 1
        keep[c], send = turn_down(order[0][1], turned, top, got[c], low[c][top], before[c], latest)
        got[c] = swap(after(send), top)
        if top == 2:
            part(c, 0, keep[c])
    for level in range(top - 1, 1, -1):
        for c in chunks:
            keep[c], send = go_down(level, keep[c], got[c], low[c][level], latest)
            got[c] = swap(after(send), level)
            if level == 2:
                part(c, 0, keep[c])
    for c in chunks:
        part(c, 1, got[c])
    out = None
    for c in chunks:
        keep[c], send = last_down(part_keep[c], part_got[c], low[c][0], latest)
        got[c] = swap(after(send), 0)
        for mine, prefix in ((True, keep[c]), (False, got[c])):
            out = finish(c, mine, queries.shape, mixed[c, mine], queries, prefix, gain, out, latest)
            latest[:] = []
        after(out, pltpu.HBM)
    return out


def solution(mesh):
    rows = P(("grp", "seq"), None)
    return jax.shard_map(
        shards, mesh=mesh, in_specs=(rows, rows, rows, P()), out_specs=rows, check_vma=False
    )
```

```python
import functools

import jax
import jax.numpy as jnp
from jax import lax
from jax.experimental import pallas as pl
from jax.experimental.pallas import tpu as pltpu
from jax.sharding import PartitionSpec as P

H = 32
E = 128
AXES = ("grp", "seq")
HALF = H // 2
CHUNKS = 2
HEADS = HALF // CHUNKS
PIECE = 4
HINT = 7 * 10**9
WIDTH = PIECE * E


def limit(mebibytes):
    return pltpu.CompilerParams(vmem_limit_bytes=mebibytes * 1024 * 1024)


def lane_tile(start, size):
    return pl.ds(pl.multiple_of(start, E), size)


def bit_of(level):
    index, length = lax.axis_index("seq"), lax.axis_size("seq")
    levels = length.bit_length() - 1
    if level < levels:
        return (index >> level) & 1
    return (lax.axis_index("grp") >> (level - levels)) & 1


def first_column(chunk, mine):
    core = bit_of(0)
    half = core if mine else 1 - core
    return (half * HALF + chunk * HEADS) * E


def load_columns(base, refs, bufs, sems):
    copies = []
    for piece in range(HEADS // PIECE):
        cols = lane_tile(base + piece * WIDTH, WIDTH)
        here = slice(piece * WIDTH, (piece + 1) * WIDTH)
        copies.append(
            [
                pltpu.make_async_copy(ref.at[:, cols], buf.at[:, here], sems.at[n, piece])
                for n, (ref, buf) in enumerate(zip(refs, bufs))
            ]
        )
        for copy in copies[-1]:
            copy.start()
    return copies


def state_kernel(chunk, mine, k_ref, v_ref, out_ref, k_out_ref, v_out_ref, sems):
    base = first_column(chunk, mine)
    copies = load_columns(base, (k_ref, v_ref), (k_out_ref, v_out_ref), sems)
    for h in range(HEADS):
        if h % PIECE == 0:
            for copy in copies[h // PIECE]:
                copy.wait()
        cols = slice(h * E, (h + 1) * E)
        out_ref[cols, :] = lax.dot_general(
            k_out_ref[:, cols],
            v_out_ref[:, cols],
            (((0,), (0,)), ((), ())),
            preferred_element_type=jnp.float32,
        )


def call(kernel, name, arrays, shapes, scratch=(), tie=(), alias=None, mebibytes=4):
    count, operands = len(arrays), list(arrays) + list(tie)

    def body(*refs):
        kernel(*refs[:count], *refs[len(operands) :])

    return pl.pallas_call(
        body,
        in_specs=[pl.BlockSpec(memory_space=space) for _, space in operands],
        out_specs=tuple(pl.BlockSpec(memory_space=space) for space, _, _ in shapes),
        out_shape=tuple(space(shape, kind) for space, shape, kind in shapes),
        scratch_shapes=scratch,
        input_output_aliases={} if alias is None else {alias: 0},
        compiler_params=limit(mebibytes),
        cost_estimate=pl.CostEstimate(flops=HINT, bytes_accessed=1, transcendentals=0),
        name=name,
    )(*[pltpu.with_memory_space_constraint(x, space) for x, space in operands])


def states_of(chunk, mine, keys, values, tie):
    columns = (pltpu.VMEM, (keys.shape[0], HEADS * E), jnp.bfloat16)
    return call(
        functools.partial(state_kernel, chunk, mine),
        "states",
        [(keys, pltpu.HBM), (values, pltpu.HBM)],
        [(pltpu.VMEM, (HEADS * E, E), jnp.float32), columns, columns],
        [pltpu.SemaphoreType.DMA((2, HEADS // PIECE))],
        tie,
        mebibytes=6,
    )


def vmem_call(kernel, name, shapes, tie, *arrays):
    return call(
        kernel,
        name,
        [(x, pltpu.VMEM) for x in arrays],
        [(pltpu.VMEM, shape, jnp.float32) for shape in shapes],
        tie=tie,
    )


def up_kernel(level, halve, keep_ref, got_ref, low_ref, *outs):
    keep, got = keep_ref[...], got_ref[...]
    low_ref[...] = jnp.where(bit_of(level) == 0, keep, got)
    total = keep + got
    if not halve:
        outs[0][...] = total
        return
    rows = total.shape[0] // 2
    one, two = total[:rows], total[rows:]
    lower = bit_of(level + 1) == 0
    outs[0][...] = jnp.where(lower, one, two)
    outs[1][...] = jnp.where(lower, two, one)


def pick(lower, one, two):
    return jnp.where(lower, one, two), jnp.where(lower, two, one)


def first_kernel(keep_ref, got_ref, low_ref, *outs):
    keep, got = keep_ref[...], got_ref[...]
    low_ref[...] = jnp.where(bit_of(0) == 0, keep, got)
    total = keep + got
    rows = total.shape[0] // 2
    mine, other = pick(bit_of(1) == 0, total[:rows], total[rows:])
    for n, half in enumerate((other, mine)):
        stays, goes_on = pick(bit_of(2) == 0, half[: rows // 2], half[rows // 2 :])
        outs[2 * n][...] = goes_on
        outs[2 * n + 1][...] = stays


def first_up(keep, got, tie):
    rows = keep.shape[0]
    shapes = [(rows, E)] + [(rows // 4, E)] * 4
    return vmem_call(first_kernel, "first_up", shapes, tie, keep, got)


def part_kernel(before_ref, low_ref, own_ref, send_ref):
    split(1, before_ref[...], low_ref[...], own_ref, send_ref)


def part_down(before, low, tie):
    return vmem_call(part_kernel, "part", [low.shape] * 2, tie, before, low)


def last_kernel(own_ref, own_on_ref, got_ref, got_on_ref, low_ref, next_ref, send_ref):
    lower = bit_of(2) == 0
    mine = jnp.concatenate(pick(lower, own_ref[...], own_on_ref[...]), axis=0)
    other = jnp.concatenate(pick(lower, got_ref[...], got_on_ref[...]), axis=0)
    before = jnp.concatenate(pick(bit_of(1) == 0, mine, other), axis=0)
    split(0, before, low_ref[...], next_ref, send_ref)


def last_down(own, got, low, tie):
    return vmem_call(last_kernel, "last_down", [low.shape] * 2, tie, *own, *got, low)


def copy_kernel(x_ref, out_ref):
    out_ref[...] = x_ref[...]


def go_up(level, halve, keep, got, tie):
    rows = keep.shape[0]
    shapes = [(rows, E)] + ([(rows // 2, E)] * 2 if halve else [(rows, E)])
    kernel = functools.partial(up_kernel, level, halve)
    return vmem_call(kernel, "up", shapes, tie, keep, got)


def group_kernel(bit, other, turned, total_ref, got_ref, before_ref, send_ref):
    total, got = total_ref[...], got_ref[...]
    before = jnp.where(bit_of(bit) == 0, 0.0, got)
    before_ref[...] = before
    if turned:
        send_ref[...] = before + jnp.where(bit_of(other) == 0, total, 0.0)
    else:
        send_ref[...] = total + got


def go_along(bit, other, turned, total, got, tie):
    kernel = functools.partial(group_kernel, bit, other, turned)
    return vmem_call(kernel, "group", [total.shape] * 2, tie, total, got)


def split(level, before, low, own_ref, send_ref):
    lower = bit_of(level) == 0
    own_ref[...] = before + jnp.where(lower, 0.0, low)
    send_ref[...] = before + jnp.where(lower, low, 0.0)


def top_kernel(bit, turned, level, got_ref, low_ref, before_ref, own_ref, send_ref):
    got = got_ref[...]
    if not turned:
        got = jnp.where(bit_of(bit) == 0, 0.0, got)
    split(level, before_ref[...] + got, low_ref[...], own_ref, send_ref)


def turn_down(bit, turned, level, got, low, before, tie):
    kernel = functools.partial(top_kernel, bit, turned, level)
    return vmem_call(kernel, "top", [low.shape] * 2, tie, got, low, before)


def down_kernel(level, own_ref, got_ref, low_ref, next_ref, send_ref):
    lower = bit_of(level + 1) == 0
    own, got = own_ref[...], got_ref[...]
    before = jnp.concatenate([jnp.where(lower, own, got), jnp.where(lower, got, own)], axis=0)
    split(level, before, low_ref[...], next_ref, send_ref)


def go_down(level, own, got, low, tie):
    kernel = functools.partial(down_kernel, level)
    return vmem_call(kernel, "down", [low.shape] * 2, tie, own, got, low)


def local_kernel(chunk, mine, q_ref, k_ref, v_ref, out_ref):
    rows = k_ref.shape[0]
    base = first_column(chunk, mine)
    causal = lax.broadcasted_iota(jnp.int32, (rows, rows), 0) >= lax.broadcasted_iota(
        jnp.int32, (rows, rows), 1
    )
    for h in range(HEADS):
        cols = slice(h * E, (h + 1) * E)
        scores = lax.dot_general(
            q_ref[:, lane_tile(base + h * E, E)],
            k_ref[:, cols],
            (((1,), (1,)), ((), ())),
            preferred_element_type=jnp.float32,
        )
        weights = jnp.where(causal, scores, 0.0).astype(jnp.bfloat16)
        out_ref[:, cols] = jnp.dot(weights, v_ref[:, cols], preferred_element_type=jnp.float32)


def local_mix(chunk, mine, queries, keys, values, tie):
    return call(
        functools.partial(local_kernel, chunk, mine),
        "local",
        [(queries, pltpu.VMEM), (keys, pltpu.VMEM), (values, pltpu.VMEM)],
        [(pltpu.VMEM, keys.shape, jnp.float32)],
        tie=tie,
        mebibytes=8,
    )[0]


def finish_kernel(chunk, mine, q_ref, m_ref, p_ref, gain_ref, *rest):
    out_ref, buf, sems = rest[-3:]
    base = first_column(chunk, mine)
    stores = []
    for piece in range(HEADS // PIECE):
        for h in range(PIECE):
            here = (piece * PIECE + h) * E
            cols = lane_tile(base + here, E)
            low = p_ref[here : here + E, :].astype(jnp.bfloat16)
            mixed = m_ref[:, here : here + E] + jnp.dot(
                q_ref[:, cols], low, preferred_element_type=jnp.float32
            )
            meansq = jnp.mean(mixed * mixed, axis=-1, keepdims=True)
            normed = mixed * lax.rsqrt(meansq + 1e-6) * gain_ref[:, cols]
            buf[piece, :, h * E : (h + 1) * E] = normed.astype(jnp.bfloat16)
        copy = pltpu.make_async_copy(
            buf.at[piece], out_ref.at[:, lane_tile(base + piece * WIDTH, WIDTH)], sems.at[piece]
        )
        copy.start()
        stores.append(copy)
    for copy in stores:
        copy.wait()


def finish(chunk, mine, shape, mixed, queries, prefix, gain, out, tie):
    pieces = HEADS // PIECE
    arrays = [(queries, pltpu.VMEM), (mixed, pltpu.VMEM), (prefix, pltpu.VMEM), (gain, pltpu.VMEM)]
    if out is not None:
        arrays.append((out, pltpu.HBM))
    return call(
        functools.partial(finish_kernel, chunk, mine),
        "finish",
        arrays,
        [(pltpu.HBM, shape, jnp.bfloat16)],
        [
            pltpu.VMEM((pieces, shape[0], WIDTH), jnp.bfloat16),
            pltpu.SemaphoreType.DMA((pieces,)),
        ],
        tie,
        None if out is None else 4,
        mebibytes=6,
    )[0]


def shards(queries, keys, values, gain):
    groups, length = lax.axis_size("grp"), lax.axis_size("seq")
    devices = groups * length
    levels = length.bit_length() - 1
    gain = gain.reshape(1, H * E)
    chunks = range(CHUNKS)

    def swap(x, level):
        return lax.ppermute(x, AXES, [(i, i ^ (1 << level)) for i in range(devices)])

    latest = []

    def after(array, space=pltpu.VMEM):
        latest[:] = [(array, space)]
        return array

    todo = [(c, mine) for c in chunks for mine in (True, False)]
    mixed, columns = {}, {}

    def some_local():
        if todo:
            this = todo.pop(0)
            mixed[this] = after(local_mix(*this, queries, *columns[this], latest))

    order = [(levels, levels + 1), (levels + 1, levels)]

    def up(level, c):
        halve = level < levels - 1
        low[c][level], keep[c], *send = go_up(level, halve, keep[c], got[c], latest)
        along = level + 1 if halve else order[c % 2][0]
        got[c] = swap(after(send[0] if halve else keep[c]), along)

    keep, got, before = [None] * CHUNKS, [None] * CHUNKS, [None] * CHUNKS
    low = [[None] * levels for _ in chunks]
    part_keep, part_got, part_low = ([[None, None] for _ in chunks] for _ in range(3))
    for c in chunks:
        send, *columns[c, False] = states_of(c, False, keys, values, latest)
        got[c] = swap(after(send), 0)
        keep[c], *columns[c, True] = states_of(c, True, keys, values, latest)
        after(keep[c])
        low[c][0], send_on, send, part_keep[c][1], part_keep[c][0] = first_up(keep[c], got[c], latest)
        part_got[c][1] = swap(after(send_on), 1)
        part_got[c][0] = swap(send, 1)
    top = levels - 1

    def goes_on(c):
        part_low[c][1], send = go_up(1, False, part_keep[c][1], part_got[c][1], latest)
        got[c] = swap(after(send), 2)

    def stays(c):
        part_low[c][0], keep[c] = go_up(1, False, part_keep[c][0], part_got[c][0], latest)
        after(keep[c])

    def along(c):
        bit, other = order[c % 2]
        before[c], send = go_along(bit, other, c % 2 == 1, keep[c], got[c], latest)
        got[c] = swap(after(send), other)

    def turn(c):
        bit, turned = order[0][1], c % 2 == 1
        keep[c], send = turn_down(bit, turned, top, got[c], low[c][top], before[c], latest)
        got[c] = swap(after(send), top)

    def part(c, n):
        whole = got[c] if n else keep[c]
        part_keep[c][n], send = part_down(whole, part_low[c][n], latest)
        part_got[c][n] = swap(after(send), 1)

    goes_on(0)
    stays(0)
    some_local()
    goes_on(1)
    up(2, 0)
    stays(1)
    some_local()
    if levels == 3:
        along(0)
        up(2, 1)
        some_local()
        turn(0)
        along(1)
        part(0, 0)
    else:
        up(2, 1)
        for level in range(3, levels):
            for c in chunks:
                up(level, c)
        for c in chunks:
            along(c)
        turn(0)
    turn(1)
    for level in range(top - 1, 1, -1):
        for c in chunks:
            keep[c], send = go_down(level, keep[c], got[c], low[c][level], latest)
            got[c] = swap(after(send), level)
    if levels > 3:
        part(0, 0)
    part(0, 1)
    part(1, 0)
    while todo:
        some_local()
    gain = after(vmem_call(copy_kernel, "gain", [gain.shape], latest, gain)[0])
    part(1, 1)
    out = None
    for c in chunks:
        keep[c], send = last_down(part_keep[c], part_got[c], low[c][0], latest)
        got[c] = swap(after(send), 0)
        for mine, prefix in ((True, keep[c]), (False, got[c])):
            out = finish(c, mine, queries.shape, mixed[c, mine], queries, prefix, gain, out, latest)
            latest[:] = []
        after(out, pltpu.HBM)
    return out


def solution(mesh):
    rows = P(("grp", "seq"), None)
    return jax.shard_map(
        shards, mesh=mesh, in_specs=(rows, rows, rows, P()), out_specs=rows, check_vma=False
    )
```

```python
import functools

import jax
import jax.numpy as jnp
from jax import lax
from jax.experimental import pallas as pl
from jax.experimental.pallas import tpu as pltpu
from jax.sharding import PartitionSpec as P

H = 32
E = 128
AXES = ("grp", "seq")
HALF = H // 2
CHUNKS = 2
HEADS = HALF // CHUNKS
PIECE = 4
OUT_PIECE = 2
HINT = 7 * 10**9
WIDTH = PIECE * E


def limit(mebibytes):
    return pltpu.CompilerParams(vmem_limit_bytes=mebibytes * 1024 * 1024)


def lane_tile(start, size):
    return pl.ds(pl.multiple_of(start, E), size)


def bit_of(level):
    index, length = lax.axis_index("seq"), lax.axis_size("seq")
    levels = length.bit_length() - 1
    if level < levels:
        return (index >> level) & 1
    return (lax.axis_index("grp") >> (level - levels)) & 1


def first_column(chunk, mine):
    core = bit_of(0)
    half = core if mine else 1 - core
    return (half * HALF + chunk * HEADS) * E


def load_columns(base, refs, bufs, sems):
    copies = []
    for piece in range(HEADS // PIECE):
        cols = lane_tile(base + piece * WIDTH, WIDTH)
        here = slice(piece * WIDTH, (piece + 1) * WIDTH)
        copies.append(
            [
                pltpu.make_async_copy(ref.at[:, cols], buf.at[:, here], sems.at[n, piece])
                for n, (ref, buf) in enumerate(zip(refs, bufs))
            ]
        )
        for copy in copies[-1]:
            copy.start()
    return copies


def state_kernel(chunk, mine, k_ref, v_ref, out_ref, k_out_ref, v_out_ref, sems):
    base = first_column(chunk, mine)
    copies = load_columns(base, (k_ref, v_ref), (k_out_ref, v_out_ref), sems)
    for h in range(HEADS):
        if h % PIECE == 0:
            for copy in copies[h // PIECE]:
                copy.wait()
        cols = slice(h * E, (h + 1) * E)
        out_ref[cols, :] = lax.dot_general(
            k_out_ref[:, cols],
            v_out_ref[:, cols],
            (((0,), (0,)), ((), ())),
            preferred_element_type=jnp.float32,
        )


def call(kernel, name, arrays, shapes, scratch=(), tie=(), alias=None, mebibytes=4):
    count, operands = len(arrays), list(arrays) + list(tie)

    def body(*refs):
        kernel(*refs[:count], *refs[len(operands) :])

    return pl.pallas_call(
        body,
        in_specs=[pl.BlockSpec(memory_space=space) for _, space in operands],
        out_specs=tuple(pl.BlockSpec(memory_space=space) for space, _, _ in shapes),
        out_shape=tuple(space(shape, kind) for space, shape, kind in shapes),
        scratch_shapes=scratch,
        input_output_aliases={} if alias is None else {alias: 0},
        compiler_params=limit(mebibytes),
        cost_estimate=pl.CostEstimate(flops=HINT, bytes_accessed=1, transcendentals=0),
        name=name,
    )(*[pltpu.with_memory_space_constraint(x, space) for x, space in operands])


def states_of(chunk, mine, keys, values, tie):
    columns = (pltpu.VMEM, (keys.shape[0], HEADS * E), jnp.bfloat16)
    return call(
        functools.partial(state_kernel, chunk, mine),
        "states",
        [(keys, pltpu.HBM), (values, pltpu.HBM)],
        [(pltpu.VMEM, (HEADS * E, E), jnp.float32), columns, columns],
        [pltpu.SemaphoreType.DMA((2, HEADS // PIECE))],
        tie,
        mebibytes=6,
    )


def vmem_call(kernel, name, shapes, tie, *arrays):
    return call(
        kernel,
        name,
        [(x, pltpu.VMEM) for x in arrays],
        [(pltpu.VMEM, shape, jnp.float32) for shape in shapes],
        tie=tie,
    )


def up_kernel(level, halve, keep_ref, got_ref, low_ref, *outs):
    keep, got = keep_ref[...], got_ref[...]
    low_ref[...] = jnp.where(bit_of(level) == 0, keep, got)
    total = keep + got
    if not halve:
        outs[0][...] = total
        return
    rows = total.shape[0] // 2
    one, two = total[:rows], total[rows:]
    lower = bit_of(level + 1) == 0
    outs[0][...] = jnp.where(lower, one, two)
    outs[1][...] = jnp.where(lower, two, one)


def pick(lower, one, two):
    return jnp.where(lower, one, two), jnp.where(lower, two, one)


def first_kernel(keep_ref, got_ref, low_ref, *outs):
    keep, got = keep_ref[...], got_ref[...]
    low_ref[...] = jnp.where(bit_of(0) == 0, keep, got)
    total = keep + got
    rows = total.shape[0] // 2
    mine, other = pick(bit_of(1) == 0, total[:rows], total[rows:])
    for n, half in enumerate((other, mine)):
        stays, goes_on = pick(bit_of(2) == 0, half[: rows // 2], half[rows // 2 :])
        outs[2 * n][...] = goes_on
        outs[2 * n + 1][...] = stays


def first_up(keep, got, tie):
    rows = keep.shape[0]
    shapes = [(rows, E)] + [(rows // 4, E)] * 4
    return vmem_call(first_kernel, "first_up", shapes, tie, keep, got)


def part_kernel(before_ref, low_ref, own_ref, send_ref):
    split(1, before_ref[...], low_ref[...], own_ref, send_ref)


def part_down(before, low, tie):
    return vmem_call(part_kernel, "part", [low.shape] * 2, tie, before, low)


def last_kernel(own_ref, own_on_ref, got_ref, got_on_ref, low_ref, next_ref, send_ref):
    lower = bit_of(2) == 0
    mine = jnp.concatenate(pick(lower, own_ref[...], own_on_ref[...]), axis=0)
    other = jnp.concatenate(pick(lower, got_ref[...], got_on_ref[...]), axis=0)
    before = jnp.concatenate(pick(bit_of(1) == 0, mine, other), axis=0)
    split(0, before, low_ref[...], next_ref, send_ref)


def last_down(own, got, low, tie):
    return vmem_call(last_kernel, "last_down", [low.shape] * 2, tie, *own, *got, low)


def copy_kernel(x_ref, out_ref):
    out_ref[...] = x_ref[...]


def go_up(level, halve, keep, got, tie):
    rows = keep.shape[0]
    shapes = [(rows, E)] + ([(rows // 2, E)] * 2 if halve else [(rows, E)])
    kernel = functools.partial(up_kernel, level, halve)
    return vmem_call(kernel, "up", shapes, tie, keep, got)


def group_kernel(bit, total_ref, got_ref, before_ref, send_ref):
    total, got = total_ref[...], got_ref[...]
    before_ref[...] = jnp.where(bit_of(bit) == 0, 0.0, got)
    send_ref[...] = total + got


def go_along(bit, total, got, tie):
    kernel = functools.partial(group_kernel, bit)
    return vmem_call(kernel, "group", [total.shape] * 2, tie, total, got)


def split(level, before, low, own_ref, send_ref):
    lower = bit_of(level) == 0
    own_ref[...] = before + jnp.where(lower, 0.0, low)
    send_ref[...] = before + jnp.where(lower, low, 0.0)


def top_kernel(bit, level, got_ref, low_ref, before_ref, own_ref, send_ref):
    before = before_ref[...] + jnp.where(bit_of(bit) == 0, 0.0, got_ref[...])
    split(level, before, low_ref[...], own_ref, send_ref)


def turn_down(bit, level, got, low, before, tie):
    kernel = functools.partial(top_kernel, bit, level)
    return vmem_call(kernel, "top", [low.shape] * 2, tie, got, low, before)


def down_kernel(level, own_ref, got_ref, low_ref, next_ref, send_ref):
    lower = bit_of(level + 1) == 0
    own, got = own_ref[...], got_ref[...]
    before = jnp.concatenate([jnp.where(lower, own, got), jnp.where(lower, got, own)], axis=0)
    split(level, before, low_ref[...], next_ref, send_ref)


def go_down(level, own, got, low, tie):
    kernel = functools.partial(down_kernel, level)
    return vmem_call(kernel, "down", [low.shape] * 2, tie, own, got, low)


def local_kernel(chunk, mine, q_ref, k_ref, v_ref, out_ref):
    rows = k_ref.shape[0]
    base = first_column(chunk, mine)
    causal = lax.broadcasted_iota(jnp.int32, (rows, rows), 0) >= lax.broadcasted_iota(
        jnp.int32, (rows, rows), 1
    )
    for h in range(HEADS):
        cols = slice(h * E, (h + 1) * E)
        scores = lax.dot_general(
            q_ref[:, lane_tile(base + h * E, E)],
            k_ref[:, cols],
            (((1,), (1,)), ((), ())),
            preferred_element_type=jnp.float32,
        )
        weights = jnp.where(causal, scores, 0.0).astype(jnp.bfloat16)
        out_ref[:, cols] = jnp.dot(weights, v_ref[:, cols], preferred_element_type=jnp.float32)


def local_mix(chunk, mine, queries, keys, values, tie):
    return call(
        functools.partial(local_kernel, chunk, mine),
        "local",
        [(queries, pltpu.VMEM), (keys, pltpu.VMEM), (values, pltpu.VMEM)],
        [(pltpu.VMEM, keys.shape, jnp.float32)],
        tie=tie,
        mebibytes=8,
    )[0]


def finish_kernel(chunk, mine, q_ref, m_ref, p_ref, gain_ref, *rest):
    out_ref, buf, sems = rest[-3:]
    base = first_column(chunk, mine)
    stores = []
    for piece in range(HEADS // OUT_PIECE):
        for h in range(OUT_PIECE):
            here = (piece * OUT_PIECE + h) * E
            cols = lane_tile(base + here, E)
            low = p_ref[here : here + E, :].astype(jnp.bfloat16)
            mixed = m_ref[:, here : here + E] + jnp.dot(
                q_ref[:, cols], low, preferred_element_type=jnp.float32
            )
            meansq = jnp.mean(mixed * mixed, axis=-1, keepdims=True)
            normed = mixed * lax.rsqrt(meansq + 1e-6) * gain_ref[:, cols]
            buf[piece, :, h * E : (h + 1) * E] = normed.astype(jnp.bfloat16)
        copy = pltpu.make_async_copy(
            buf.at[piece], out_ref.at[:, lane_tile(base + piece * OUT_PIECE * E, OUT_PIECE * E)], sems.at[piece]
        )
        copy.start()
        stores.append(copy)
    for copy in stores:
        copy.wait()


def finish(chunk, mine, shape, mixed, queries, prefix, gain, out, tie):
    pieces = HEADS // OUT_PIECE
    arrays = [(queries, pltpu.VMEM), (mixed, pltpu.VMEM), (prefix, pltpu.VMEM), (gain, pltpu.VMEM)]
    if out is not None:
        arrays.append((out, pltpu.HBM))
    return call(
        functools.partial(finish_kernel, chunk, mine),
        "finish",
        arrays,
        [(pltpu.HBM, shape, jnp.bfloat16)],
        [
            pltpu.VMEM((pieces, shape[0], OUT_PIECE * E), jnp.bfloat16),
            pltpu.SemaphoreType.DMA((pieces,)),
        ],
        tie,
        None if out is None else 4,
        mebibytes=6,
    )[0]


def shards(queries, keys, values, gain):
    groups, length = lax.axis_size("grp"), lax.axis_size("seq")
    devices = groups * length
    levels = length.bit_length() - 1
    gain = gain.reshape(1, H * E)
    chunks = range(CHUNKS)

    def swap(x, level):
        return lax.ppermute(x, AXES, [(i, i ^ (1 << level)) for i in range(devices)])

    latest = []

    def after(array, space=pltpu.VMEM):
        latest[:] = [(array, space)]
        return array

    todo = [(c, mine) for c in chunks for mine in (True, False)]
    mixed, columns = {}, {}

    def some_local():
        if todo:
            this = todo.pop(0)
            mixed[this] = after(local_mix(*this, queries, *columns[this], latest))

    def up(level, c):
        halve = level < levels - 1
        low[c][level], keep[c], *send = go_up(level, halve, keep[c], got[c], latest)
        got[c] = swap(after(send[0] if halve else keep[c]), level + 1)

    keep, got, before = [None] * CHUNKS, [None] * CHUNKS, [None] * CHUNKS
    low = [[None] * levels for _ in chunks]
    part_keep, part_got, part_low = ([[None, None] for _ in chunks] for _ in range(3))
    for c in chunks:
        send, *columns[c, False] = states_of(c, False, keys, values, latest)
        got[c] = swap(after(send), 0)
        keep[c], *columns[c, True] = states_of(c, True, keys, values, latest)
        after(keep[c])
        low[c][0], send_on, send, part_keep[c][1], part_keep[c][0] = first_up(keep[c], got[c], latest)
        part_got[c][1] = swap(after(send_on), 1)
        part_got[c][0] = swap(send, 1)
    top = levels - 1

    def goes_on(c):
        part_low[c][1], send = go_up(1, False, part_keep[c][1], part_got[c][1], latest)
        got[c] = swap(after(send), 2)

    def stays(c):
        part_low[c][0], keep[c] = go_up(1, False, part_keep[c][0], part_got[c][0], latest)
        after(keep[c])

    def along(c):
        before[c], send = go_along(levels, keep[c], got[c], latest)
        got[c] = swap(after(send), levels + 1)

    def turn(c):
        keep[c], send = turn_down(levels + 1, top, got[c], low[c][top], before[c], latest)
        got[c] = swap(after(send), top)

    def part(c, n):
        whole = got[c] if n else keep[c]
        part_keep[c][n], send = part_down(whole, part_low[c][n], latest)
        part_got[c][n] = swap(after(send), 1)

    goes_on(0)
    stays(0)
    some_local()
    goes_on(1)
    up(2, 0)
    stays(1)
    some_local()
    if levels == 3:
        along(0)
        up(2, 1)
        some_local()
        turn(0)
        along(1)
        part(0, 0)
    else:
        up(2, 1)
        for level in range(3, levels):
            for c in chunks:
                up(level, c)
        for c in chunks:
            along(c)
        turn(0)
    turn(1)
    for level in range(top - 1, 1, -1):
        for c in chunks:
            keep[c], send = go_down(level, keep[c], got[c], low[c][level], latest)
            got[c] = swap(after(send), level)
    if levels > 3:
        part(0, 0)
    part(0, 1)
    part(1, 0)
    while todo:
        some_local()
    gain = after(vmem_call(copy_kernel, "gain", [gain.shape], latest, gain)[0])
    def last(c):
        keep[c], send = last_down(part_keep[c], part_got[c], low[c][0], latest)
        got[c] = swap(after(send), 0)

    part(1, 1)
    out = None
    for c in chunks:
        last(c)
        for mine, prefix in ((True, keep[c]), (False, got[c])):
            out = finish(c, mine, queries.shape, mixed[c, mine], queries, prefix, gain, out, latest)
            latest[:] = []
        after(out, pltpu.HBM)
    return out


def solution(mesh):
    rows = P(("grp", "seq"), None)
    return jax.shard_map(
        shards, mesh=mesh, in_specs=(rows, rows, rows, P()), out_specs=rows, check_vma=False
    )
```

```python
import functools

import jax
import jax.numpy as jnp
from jax import lax
from jax.experimental import pallas as pl
from jax.experimental.pallas import tpu as pltpu
from jax.sharding import PartitionSpec as P

H = 32
E = 128
AXES = ("grp", "seq")
HALF = H // 2
CHUNKS = 2
HEADS = HALF // CHUNKS
PIECE = 4
OUT_PIECE = 2
HINT = 7 * 10**9
HINTS = {"up": 10**9}
WIDTH = PIECE * E


def limit(mebibytes):
    return pltpu.CompilerParams(vmem_limit_bytes=mebibytes * 1024 * 1024)


def lane_tile(start, size):
    return pl.ds(pl.multiple_of(start, E), size)


def bit_of(level):
    index, length = lax.axis_index("seq"), lax.axis_size("seq")
    levels = length.bit_length() - 1
    if level < levels:
        return (index >> level) & 1
    return (lax.axis_index("grp") >> (level - levels)) & 1


def first_column(chunk, mine):
    core = bit_of(0)
    half = core if mine else 1 - core
    return (half * HALF + chunk * HEADS) * E


def load_columns(base, refs, bufs, sems):
    copies = []
    for piece in range(HEADS // PIECE):
        cols = lane_tile(base + piece * WIDTH, WIDTH)
        here = slice(piece * WIDTH, (piece + 1) * WIDTH)
        copies.append(
            [
                pltpu.make_async_copy(ref.at[:, cols], buf.at[:, here], sems.at[n, piece])
                for n, (ref, buf) in enumerate(zip(refs, bufs))
            ]
        )
        for copy in copies[-1]:
            copy.start()
    return copies


def state_kernel(chunk, mine, k_ref, v_ref, out_ref, k_out_ref, v_out_ref, sems):
    base = first_column(chunk, mine)
    copies = load_columns(base, (k_ref, v_ref), (k_out_ref, v_out_ref), sems)
    for h in range(HEADS):
        if h % PIECE == 0:
            for copy in copies[h // PIECE]:
                copy.wait()
        cols = slice(h * E, (h + 1) * E)
        out_ref[cols, :] = lax.dot_general(
            k_out_ref[:, cols],
            v_out_ref[:, cols],
            (((0,), (0,)), ((), ())),
            preferred_element_type=jnp.float32,
        )


def call(kernel, name, arrays, shapes, scratch=(), tie=(), alias=None, mebibytes=4):
    count, operands = len(arrays), list(arrays) + list(tie)

    def body(*refs):
        kernel(*refs[:count], *refs[len(operands) :])

    return pl.pallas_call(
        body,
        in_specs=[pl.BlockSpec(memory_space=space) for _, space in operands],
        out_specs=tuple(pl.BlockSpec(memory_space=space) for space, _, _ in shapes),
        out_shape=tuple(space(shape, kind) for space, shape, kind in shapes),
        scratch_shapes=scratch,
        input_output_aliases={} if alias is None else {alias: 0},
        compiler_params=limit(mebibytes),
        cost_estimate=pl.CostEstimate(flops=HINTS.get(name, HINT), bytes_accessed=1, transcendentals=0),
        name=name,
    )(*[pltpu.with_memory_space_constraint(x, space) for x, space in operands])


def states_of(chunk, mine, keys, values, tie):
    columns = (pltpu.VMEM, (keys.shape[0], HEADS * E), jnp.bfloat16)
    return call(
        functools.partial(state_kernel, chunk, mine),
        "states",
        [(keys, pltpu.HBM), (values, pltpu.HBM)],
        [(pltpu.VMEM, (HEADS * E, E), jnp.float32), columns, columns],
        [pltpu.SemaphoreType.DMA((2, HEADS // PIECE))],
        tie,
        mebibytes=6,
    )


def vmem_call(kernel, name, shapes, tie, *arrays):
    return call(
        kernel,
        name,
        [(x, pltpu.VMEM) for x in arrays],
        [(pltpu.VMEM, shape, jnp.float32) for shape in shapes],
        tie=tie,
    )


def up_kernel(level, halve, keep_ref, got_ref, low_ref, *outs):
    keep, got = keep_ref[...], got_ref[...]
    low_ref[...] = jnp.where(bit_of(level) == 0, keep, got)
    total = keep + got
    if not halve:
        outs[0][...] = total
        return
    rows = total.shape[0] // 2
    one, two = total[:rows], total[rows:]
    lower = bit_of(level + 1) == 0
    outs[0][...] = jnp.where(lower, one, two)
    outs[1][...] = jnp.where(lower, two, one)


def pick(lower, one, two):
    return jnp.where(lower, one, two), jnp.where(lower, two, one)


def first_kernel(keep_ref, got_ref, low_ref, *outs):
    keep, got = keep_ref[...], got_ref[...]
    low_ref[...] = jnp.where(bit_of(0) == 0, keep, got)
    total = keep + got
    rows = total.shape[0] // 2
    mine, other = pick(bit_of(1) == 0, total[:rows], total[rows:])
    for n, half in enumerate((other, mine)):
        stays, goes_on = pick(bit_of(2) == 0, half[: rows // 2], half[rows // 2 :])
        outs[2 * n][...] = goes_on
        outs[2 * n + 1][...] = stays


def first_up(keep, got, tie):
    rows = keep.shape[0]
    shapes = [(rows, E)] + [(rows // 4, E)] * 4
    return vmem_call(first_kernel, "first_up", shapes, tie, keep, got)


def part_kernel(before_ref, low_ref, own_ref, send_ref):
    split(1, before_ref[...], low_ref[...], own_ref, send_ref)


def part_down(before, low, tie):
    return vmem_call(part_kernel, "part", [low.shape] * 2, tie, before, low)


def last_kernel(own_ref, own_on_ref, got_ref, got_on_ref, low_ref, next_ref, send_ref):
    lower = bit_of(2) == 0
    mine = jnp.concatenate(pick(lower, own_ref[...], own_on_ref[...]), axis=0)
    other = jnp.concatenate(pick(lower, got_ref[...], got_on_ref[...]), axis=0)
    before = jnp.concatenate(pick(bit_of(1) == 0, mine, other), axis=0)
    split(0, before, low_ref[...], next_ref, send_ref)


def last_down(own, got, low, tie):
    return vmem_call(last_kernel, "last_down", [low.shape] * 2, tie, *own, *got, low)


def copy_kernel(x_ref, out_ref):
    out_ref[...] = x_ref[...]


def go_up(level, halve, keep, got, tie):
    rows = keep.shape[0]
    shapes = [(rows, E)] + ([(rows // 2, E)] * 2 if halve else [(rows, E)])
    kernel = functools.partial(up_kernel, level, halve)
    return vmem_call(kernel, "up", shapes, tie, keep, got)


def group_kernel(bit, total_ref, got_ref, before_ref, send_ref):
    total, got = total_ref[...], got_ref[...]
    before_ref[...] = jnp.where(bit_of(bit) == 0, 0.0, got)
    send_ref[...] = total + got


def go_along(bit, total, got, tie):
    kernel = functools.partial(group_kernel, bit)
    return vmem_call(kernel, "group", [total.shape] * 2, tie, total, got)


def split(level, before, low, own_ref, send_ref):
    lower = bit_of(level) == 0
    own_ref[...] = before + jnp.where(lower, 0.0, low)
    send_ref[...] = before + jnp.where(lower, low, 0.0)


def top_kernel(bit, level, got_ref, low_ref, before_ref, own_ref, send_ref):
    before = before_ref[...] + jnp.where(bit_of(bit) == 0, 0.0, got_ref[...])
    split(level, before, low_ref[...], own_ref, send_ref)


def turn_down(bit, level, got, low, before, tie):
    kernel = functools.partial(top_kernel, bit, level)
    return vmem_call(kernel, "top", [low.shape] * 2, tie, got, low, before)


def down_kernel(level, own_ref, got_ref, low_ref, next_ref, send_ref):
    lower = bit_of(level + 1) == 0
    own, got = own_ref[...], got_ref[...]
    before = jnp.concatenate([jnp.where(lower, own, got), jnp.where(lower, got, own)], axis=0)
    split(level, before, low_ref[...], next_ref, send_ref)


def go_down(level, own, got, low, tie):
    kernel = functools.partial(down_kernel, level)
    return vmem_call(kernel, "down", [low.shape] * 2, tie, own, got, low)


def local_kernel(chunk, mine, q_ref, k_ref, v_ref, out_ref):
    rows = k_ref.shape[0]
    base = first_column(chunk, mine)
    causal = lax.broadcasted_iota(jnp.int32, (rows, rows), 0) >= lax.broadcasted_iota(
        jnp.int32, (rows, rows), 1
    )
    for h in range(HEADS):
        cols = slice(h * E, (h + 1) * E)
        scores = lax.dot_general(
            q_ref[:, lane_tile(base + h * E, E)],
            k_ref[:, cols],
            (((1,), (1,)), ((), ())),
            preferred_element_type=jnp.float32,
        )
        weights = jnp.where(causal, scores, 0.0).astype(jnp.bfloat16)
        out_ref[:, cols] = jnp.dot(weights, v_ref[:, cols], preferred_element_type=jnp.float32)


def local_mix(chunk, mine, queries, keys, values, tie):
    return call(
        functools.partial(local_kernel, chunk, mine),
        "local",
        [(queries, pltpu.VMEM), (keys, pltpu.VMEM), (values, pltpu.VMEM)],
        [(pltpu.VMEM, keys.shape, jnp.float32)],
        tie=tie,
        mebibytes=8,
    )[0]


def finish_kernel(chunk, mine, q_ref, m_ref, p_ref, gain_ref, *rest):
    out_ref, buf, sems = rest[-3:]
    base = first_column(chunk, mine)
    stores = []
    for piece in range(HEADS // OUT_PIECE):
        for h in range(OUT_PIECE):
            here = (piece * OUT_PIECE + h) * E
            cols = lane_tile(base + here, E)
            low = p_ref[here : here + E, :].astype(jnp.bfloat16)
            mixed = m_ref[:, here : here + E] + jnp.dot(
                q_ref[:, cols], low, preferred_element_type=jnp.float32
            )
            meansq = jnp.mean(mixed * mixed, axis=-1, keepdims=True)
            normed = mixed * lax.rsqrt(meansq + 1e-6) * gain_ref[:, cols]
            buf[piece, :, h * E : (h + 1) * E] = normed.astype(jnp.bfloat16)
        copy = pltpu.make_async_copy(
            buf.at[piece], out_ref.at[:, lane_tile(base + piece * OUT_PIECE * E, OUT_PIECE * E)], sems.at[piece]
        )
        copy.start()
        stores.append(copy)
    for copy in stores:
        copy.wait()


def finish(chunk, mine, shape, mixed, queries, prefix, gain, out, tie):
    pieces = HEADS // OUT_PIECE
    arrays = [(queries, pltpu.VMEM), (mixed, pltpu.VMEM), (prefix, pltpu.VMEM), (gain, pltpu.VMEM)]
    if out is not None:
        arrays.append((out, pltpu.HBM))
    return call(
        functools.partial(finish_kernel, chunk, mine),
        "finish",
        arrays,
        [(pltpu.HBM, shape, jnp.bfloat16)],
        [
            pltpu.VMEM((pieces, shape[0], OUT_PIECE * E), jnp.bfloat16),
            pltpu.SemaphoreType.DMA((pieces,)),
        ],
        tie,
        None if out is None else 4,
        mebibytes=6,
    )[0]


def shards(queries, keys, values, gain):
    groups, length = lax.axis_size("grp"), lax.axis_size("seq")
    devices = groups * length
    levels = length.bit_length() - 1
    gain = gain.reshape(1, H * E)
    chunks = range(CHUNKS)

    def swap(x, level):
        return lax.ppermute(x, AXES, [(i, i ^ (1 << level)) for i in range(devices)])

    latest = []

    def after(array, space=pltpu.VMEM):
        latest[:] = [(array, space)]
        return array

    todo = [(c, mine) for c in chunks for mine in (True, False)]
    mixed, columns = {}, {}

    def some_local():
        if todo:
            this = todo.pop(0)
            mixed[this] = after(local_mix(*this, queries, *columns[this], latest))

    def up(level, c):
        halve = level < levels - 1
        low[c][level], keep[c], *send = go_up(level, halve, keep[c], got[c], latest)
        got[c] = swap(after(send[0] if halve else keep[c]), level + 1)

    keep, got, before = [None] * CHUNKS, [None] * CHUNKS, [None] * CHUNKS
    low = [[None] * levels for _ in chunks]
    part_keep, part_got, part_low = ([[None, None] for _ in chunks] for _ in range(3))
    for c in chunks:
        send, *columns[c, False] = states_of(c, False, keys, values, latest)
        got[c] = swap(after(send), 0)
        keep[c], *columns[c, True] = states_of(c, True, keys, values, latest)
        after(keep[c])
        low[c][0], send_on, send, part_keep[c][1], part_keep[c][0] = first_up(keep[c], got[c], latest)
        part_got[c][1] = swap(after(send_on), 1)
        part_got[c][0] = swap(send, 1)
    top = levels - 1

    def goes_on(c):
        part_low[c][1], send = go_up(1, False, part_keep[c][1], part_got[c][1], latest)
        got[c] = swap(after(send), 2)

    def stays(c):
        part_low[c][0], keep[c] = go_up(1, False, part_keep[c][0], part_got[c][0], latest)
        after(keep[c])

    def along(c):
        before[c], send = go_along(levels, keep[c], got[c], latest)
        got[c] = swap(after(send), levels + 1)

    def turn(c):
        keep[c], send = turn_down(levels + 1, top, got[c], low[c][top], before[c], latest)
        got[c] = swap(after(send), top)

    def part(c, n):
        whole = got[c] if n else keep[c]
        part_keep[c][n], send = part_down(whole, part_low[c][n], latest)
        part_got[c][n] = swap(after(send), 1)

    goes_on(0)
    stays(0)
    some_local()
    some_local()
    goes_on(1)
    up(2, 0)
    stays(1)
    some_local()
    if levels == 3:
        along(0)
        up(2, 1)
        turn(0)
        along(1)
        part(0, 0)
    else:
        up(2, 1)
        for level in range(3, levels):
            for c in chunks:
                up(level, c)
        for c in chunks:
            along(c)
        turn(0)
    turn(1)
    for level in range(top - 1, 1, -1):
        for c in chunks:
            keep[c], send = go_down(level, keep[c], got[c], low[c][level], latest)
            got[c] = swap(after(send), level)
    if levels > 3:
        part(0, 0)
    part(0, 1)
    while todo:
        some_local()
    gain = after(vmem_call(copy_kernel, "gain", [gain.shape], latest, gain)[0])
    def last(c):
        keep[c], send = last_down(part_keep[c], part_got[c], low[c][0], latest)
        got[c] = swap(after(send), 0)

    part(1, 0)
    part(1, 1)
    out = None
    for c in chunks:
        last(c)
        for mine, prefix in ((True, keep[c]), (False, got[c])):
            out = finish(c, mine, queries.shape, mixed[c, mine], queries, prefix, gain, out, latest)
            latest[:] = []
        after(out, pltpu.HBM)
    return out


def solution(mesh):
    rows = P(("grp", "seq"), None)
    return jax.shard_map(
        shards, mesh=mesh, in_specs=(rows, rows, rows, P()), out_specs=rows, check_vma=False
    )
```
